256 devices in a mesh: gx: 64 (over z, x, core), gy: 4 (over y).
Axes of the slice: x: 4, y: 4, z: 8, core: 2. Of those that a mesh axis runs over, the one named last changes fastest.
Arguments:
- embeddings: bfloat16 [262144, 768], P(('gx', 'gy')), may hold values from -12 to 12
- clusters: int32 [262144], P(('gx', 'gy')), may hold values from 0 to 511, as said below
- priorities: int32 [262144], P(('gx', 'gy')), may hold values from 0 to 262143, each once
Outputs:
- best_similarity: float32 [262144], P(('gx', 'gy'))
The draws below stay inside these ranges and needn't reach their ends.
Inputs may be any that keep to these rules, and one draw needn't show every extreme that they name: For every o, the rows of one device name the 2 clusters c with c // 2 == o at most 6 times together; one cluster, drawn from the seed, is named exactly 6 times by the rows of every device. `priorities`: all distinct.
All inputs are finite; a program needn't handle non-finite values.
Results may differ from the reference program's by a relative error of at most 0.0003.
Values may be sent and summed in bfloat16 or wider, within the bound.
No kernel may reach another device: no remote copies, remote signals or barrier semaphores. Data moves between devices by JAX's collectives and lax.ppermute only.
A program may use at most 128 MiB of HBM per device.

```python
import jax
import jax.numpy as jnp
from jax import lax

D = 768
CLUS_DEV = 2
ROWS_DEV = 1024
CLUSTERS = 512
OWN_CAP = 6
ROWS = 262144
N_GX = 64
N_GY = 4


def cluster_labels(key):
    nblocks = ROWS // ROWS_DEV
    owner_count = CLUSTERS // CLUS_DEV
    slot_count = owner_count * OWN_CAP
    first, second, third, fourth, fifth = jax.random.split(key, 5)
    chosen_hot = jax.random.randint(first, (), 0, CLUSTERS)
    busiest_owner = chosen_hot // CLUS_DEV
    heat_level = jax.random.randint(second, (owner_count,), 0, 2 ** 14)
    random_perturbation = jax.random.randint(third, (nblocks, slot_count), 0, 2 ** 14)
    slot_holder = jnp.arange(slot_count, dtype=jnp.int32) // OWN_CAP
    extra_reward = jnp.where(slot_holder == busiest_owner, 2 ** 16, 0).astype(jnp.int32)
    baseline_load = random_perturbation + heat_level[slot_holder][None, :] + extra_reward[None, :]
    score = baseline_load * slot_count + jnp.arange(slot_count, dtype=jnp.int32)[None, :]
    ignored, picked = lax.top_k(score, ROWS_DEV)
    shuffle = jax.vmap(lambda block_key: jax.random.permutation(block_key, ROWS_DEV))(jax.random.split(fourth, nblocks))
    picked = jnp.take_along_axis(picked, shuffle, axis=1).reshape(-1)
    owner = picked // OWN_CAP
    member = jax.random.randint(fifth, (nblocks * ROWS_DEV,), 0, CLUS_DEV)
    labels = jnp.where(owner == busiest_owner, chosen_hot, owner * CLUS_DEV + member)
    return labels.astype(jnp.int32)


def draw_clusters(key, part):
    return cluster_labels(key)


def draw_embeddings(key, part):
    labels = cluster_labels(key)
    key = jax.random.fold_in(key, 11)
    first, second, third = jax.random.split(key, 3)
    centers = jax.random.normal(first, (CLUSTERS, D), jnp.float32)
    noise = jax.random.normal(second, (ROWS, D), jnp.float32)
    strength = jax.random.uniform(third, (ROWS, 1), jnp.float32, 0.3, 2.0)
    values = strength * centers[labels] + noise
    return jnp.clip(values, -12.0, 12.0).astype(jnp.bfloat16)


def setup_inputs(seed: int = 0) -> dict:
    key_of = jax.random.split(jax.random.key(seed), 4)
    return {
        "embeddings": draw_embeddings(jax.random.fold_in(key_of[3], 71), 0),
        "clusters": draw_clusters(jax.random.fold_in(key_of[3], 71), 0),
        "priorities": jax.random.permutation(key_of[2], ROWS).astype(jnp.int32),
    }


norm_eps = 1e-06

def inverse_norm(values):
    wide = values.astype(jnp.float32)
    return lax.rsqrt(lax.optimization_barrier(jnp.sum(wide * wide, axis=-1)) + norm_eps)

def reference(embeddings, clusters, priorities):
    total = clusters.shape[0]
    most = OWN_CAP * N_GX * N_GY
    sort_key = clusters * total + priorities
    order = jnp.argsort(sort_key).astype(jnp.int32)
    sorted_rows = embeddings[order]
    sorted_labels = clusters[order]
    sorted_ranks = priorities[order]
    sorted_scale = inverse_norm(sorted_rows)
    padded_rows = jnp.concatenate([jnp.zeros((most, D), embeddings.dtype), sorted_rows], axis=0)
    padded_labels = jnp.concatenate([jnp.full((most,), -1, jnp.int32), sorted_labels], axis=0)
    padded_ranks = jnp.concatenate([jnp.zeros((most,), jnp.int32), sorted_ranks], axis=0)
    padded_scale = jnp.concatenate([jnp.zeros((most,), jnp.float32), sorted_scale], axis=0)
    block = 512

    def single_block(number):
        begin = (number * block).astype(jnp.int32)
        query_rows = lax.dynamic_slice_in_dim(sorted_rows, begin, block, 0)
        query_labels = lax.dynamic_slice_in_dim(sorted_labels, begin, block, 0)
        query_ranks = lax.dynamic_slice_in_dim(sorted_ranks, begin, block, 0)
        query_scale = lax.dynamic_slice_in_dim(sorted_scale, begin, block, 0)
        window = most + block
        key_rows = lax.dynamic_slice_in_dim(padded_rows, begin, window, 0)
        key_labels = lax.dynamic_slice_in_dim(padded_labels, begin, window, 0)
        key_ranks = lax.dynamic_slice_in_dim(padded_ranks, begin, window, 0)
        key_scale = lax.dynamic_slice_in_dim(padded_scale, begin, window, 0)
        scores = jnp.dot(query_rows, key_rows.T, preferred_element_type=jnp.float32)
        scores = scores * query_scale[:, None] * key_scale[None, :]
        allowed = (key_labels[None, :] == query_labels[:, None]) & (key_ranks[None, :] < query_ranks[:, None])
        return lax.optimization_barrier(jnp.max(jnp.where(allowed, scores, -1.0), axis=1))
    blocks_best = lax.map(single_block, jnp.arange(total // block, dtype=jnp.int32))
    flat_best = blocks_best.reshape(-1)
    return jnp.zeros((total,), jnp.float32).at[order].set(flat_best)
```

```python
import functools

import jax
import jax.numpy as jnp
from jax import lax
from jax.experimental import pallas as pl
from jax.experimental.pallas import tpu as pltpu
from jax.sharding import PartitionSpec as P

CLUS_DEV = 2
OWN_CAP = 6
LANES = 128
META = 2
DIGIT = 128

norm_eps = 1e-06
bf16 = jnp.bfloat16
f32 = jnp.float32


def iota(shape, dim):
    return lax.broadcasted_iota(jnp.int32, shape, dim)


def pack_kernel(label_span, c_ref, p_ref, x_ref, w_ref, slot_ref, wide_ref):
    owners, rows = slot_ref.shape
    width = x_ref.shape[1]
    parts = width // LANES
    stride = w_ref.shape[0] // owners
    block = min(256, rows)
    clusters = c_ref[...]
    owner = clusters // CLUS_DEV
    key = (clusters % CLUS_DEV) * label_span + p_ref[...] + 1
    before = (iota((block, block), 0) < iota((block, block), 1)).astype(f32).astype(bf16)
    carry = jnp.zeros((owners, 1), f32)
    for b in range(rows // block):
        cols = slice(b * block, (b + 1) * block)
        named = iota((owners, block), 0) == owner[:, cols]
        ones = named.astype(f32)
        rank = jnp.dot(ones.astype(bf16), before, preferred_element_type=f32) + carry
        slot_ref[:, cols] = jnp.where(named, rank, -1.0)
        carry = carry + jnp.sum(ones, axis=1, keepdims=True)
    kind = iota((LANES, rows), 0) % 8
    digits = jnp.where(
        kind == 0,
        key % DIGIT,
        jnp.where(kind == 1, key // DIGIT % DIGIT, jnp.where(kind == 2, key // DIGIT**2, 0)),
    )
    digits = digits.astype(f32).astype(bf16)
    lane = iota((owners, LANES), 1) // 8
    meta = jnp.zeros((owners, LANES), f32)
    for q in range(OWN_CAP):
        pick = (slot_ref[...] == q).astype(f32).astype(bf16)
        picked = jnp.dot(pick, x_ref[...], preferred_element_type=f32)
        for k in range(parts):
            wide_ref[pl.ds(q * parts + k, owners, stride=stride), :] = picked[
                :, k * LANES : (k + 1) * LANES
            ]
        digit = lax.dot_general(
            pick, digits, (((1,), (1,)), ((), ())), preferred_element_type=f32
        )
        meta = jnp.where(lane == q, digit, meta)
    wide_ref[pl.ds(OWN_CAP * parts, owners, stride=stride), :] = meta
    wide_ref[pl.ds(OWN_CAP * parts + 1, owners, stride=stride), :] = jnp.zeros_like(meta)
    w_ref[...] = wide_ref[...].astype(bf16)


def score_kernel(label_span, w_ref, out_ref, wide_ref, x_ref):
    sources = out_ref.shape[0]
    width = x_ref.shape[1]
    parts = width // LANES
    stride = w_ref.shape[0] // sources
    wide_ref[...] = w_ref[...].astype(f32)
    meta = wide_ref[pl.ds(OWN_CAP * parts, sources, stride=stride), :]
    lane = iota((sources, LANES), 1)
    table = jnp.zeros((sources, LANES), f32)
    keys, scales = [], []
    for r in range(OWN_CAP):
        squares = jnp.zeros((sources, LANES), f32)
        for k in range(parts):
            part = wide_ref[pl.ds(r * parts + k, sources, stride=stride), :]
            x_ref[r * sources : (r + 1) * sources, k * LANES : (k + 1) * LANES] = part.astype(bf16)
            squares = squares + part * part
        scale = lax.rsqrt(jnp.sum(squares, axis=1, keepdims=True) + norm_eps)
        key = (
            meta[:, 8 * r : 8 * r + 1]
            + DIGIT * meta[:, 8 * r + 1 : 8 * r + 2]
            + DIGIT**2 * meta[:, 8 * r + 2 : 8 * r + 3]
        )
        keys.append(key)
        scales.append(scale)
        table = jnp.where(lane == r, key, jnp.where(lane == r + 8, scale, table))
    turned = table.T
    result = jnp.full((sources, LANES), -1.0, f32)
    for r in range(OWN_CAP):
        query = x_ref[r * sources : (r + 1) * sources, :]
        low = jnp.where(keys[r] > label_span, float(label_span), 0.0)
        best = jnp.full((sources, sources), -jnp.inf, f32)
        for t in range(OWN_CAP):
            scores = lax.dot_general(
                query,
                x_ref[t * sources : (t + 1) * sources, :],
                (((1,), (1,)), ((), ())),
                preferred_element_type=f32,
            )
            scores = scores * turned[t + 8 : t + 9, :]
            other = turned[t : t + 1, :]
            allowed = (other < keys[r]) & (other > low)
            best = jnp.maximum(best, jnp.where(allowed, scores, -jnp.inf))
        top = jnp.max(best, axis=1, keepdims=True) * scales[r]
        result = jnp.where(lane == r, jnp.maximum(top, -1.0), result)
    out_ref[...] = result[:, :OWN_CAP]


def pick_kernel(r_ref, slot_ref, out_ref):
    slot = slot_ref[...]
    value = jnp.zeros(slot.shape, f32)
    for q in range(OWN_CAP):
        value = jnp.where(slot == q, r_ref[:, q : q + 1], value)
    out_ref[...] = jnp.sum(value, axis=0, keepdims=True)


def call(kernel, out_shape, scratch, name):
    return pl.pallas_call(
        kernel,
        out_shape=out_shape,
        scratch_shapes=scratch,
        compiler_params=pltpu.CompilerParams(vmem_limit_bytes=48 * 2**20),
        name=name,
    )


def shards(embeddings, clusters, priorities):
    rows, width = embeddings.shape
    owners = lax.axis_size("gx") * lax.axis_size("gy")
    label_span = rows * owners
    height = owners * (OWN_CAP * width // LANES + META)
    wide = pltpu.VMEM((height, LANES), f32)
    packed, slot = call(
        functools.partial(pack_kernel, label_span),
        (
            jax.ShapeDtypeStruct((height, LANES), bf16),
            jax.ShapeDtypeStruct((owners, rows), f32),
        ),
        [wide],
        "pack",
    )(clusters.reshape(1, rows), priorities.reshape(1, rows), embeddings)
    arrived = lax.all_to_all(
        packed.reshape(owners, height // owners // 2, 2, LANES),
        ("gx", "gy"),
        split_axis=0,
        concat_axis=0,
        tiled=True,
    ).reshape(height, LANES)
    result = call(
        functools.partial(score_kernel, label_span),
        jax.ShapeDtypeStruct((owners, OWN_CAP), f32),
        [wide, pltpu.VMEM((OWN_CAP * owners, width), bf16)],
        "score",
    )(arrived)
    returned = lax.all_to_all(result, ("gx", "gy"), split_axis=0, concat_axis=0, tiled=True)
    best = call(pick_kernel, jax.ShapeDtypeStruct((1, rows), f32), [], "pick")(returned, slot)
    return best.reshape(rows)


def solution(mesh):
    in_specs = (P(("gx", "gy"), None), P(("gx", "gy")), P(("gx", "gy")))
    out_specs = P(("gx", "gy"))
    return jax.shard_map(shards, mesh=mesh, in_specs=in_specs, out_specs=out_specs, check_vma=False)
```

```python
import functools

import jax
import jax.numpy as jnp
from jax import lax
from jax.experimental import pallas as pl
from jax.experimental.pallas import tpu as pltpu
from jax.sharding import PartitionSpec as P

CLUS_DEV = 2
OWN_CAP = 6
LANES = 128
META = 2
DIGIT = 128
X_PIECES = 1
STEP = 32

norm_eps = 1e-06
bf16 = jnp.bfloat16
f32 = jnp.float32


def iota(shape, dim):
    return lax.broadcasted_iota(jnp.int32, shape, dim)


def pack_kernel(
    label_span, c_hbm, p_hbm, x_hbm, w_ref, slot_ref, wide_ref, c_ref, p_ref, x_ref, sems
):
    owners, rows = slot_ref.shape
    width = x_ref.shape[1]
    parts = width // LANES
    stride = w_ref.shape[0] // owners
    block = min(256, rows)
    copies = [
        pltpu.make_async_copy(c_hbm, c_ref, sems.at[0]),
        pltpu.make_async_copy(p_hbm, p_ref, sems.at[1]),
    ]
    piece = rows // X_PIECES
    for i in range(X_PIECES):
        span = pl.ds(i * piece, piece)
        copies.append(pltpu.make_async_copy(x_hbm.at[span], x_ref.at[span], sems.at[2 + i]))
    for copy in copies:
        copy.start()
    before = (iota((block, block), 0) < iota((block, block), 1)).astype(f32).astype(bf16)
    copies[0].wait()
    copies[1].wait()
    clusters = c_ref[...]
    owner = clusters // CLUS_DEV
    key = (clusters % CLUS_DEV) * label_span + p_ref[...] + 1
    ones = jnp.ones((block, block), bf16)
    earlier = None
    for b in range(rows // block):
        cols = slice(b * block, (b + 1) * block)
        named = iota((owners, block), 0) == owner[:, cols]
        count = named.astype(f32).astype(bf16)
        rank = jnp.dot(count, before, preferred_element_type=f32)
        if b:
            rank = rank + jnp.dot(earlier, ones, preferred_element_type=f32)
        earlier = earlier + count if b else count
        slot_ref[:, cols] = jnp.where(named, rank, -1.0)
    key = key.astype(f32)
    lane = iota((owners, LANES), 1)
    table = jnp.zeros((owners, LANES), f32)
    for copy in copies[2:]:
        copy.wait()
    for q in range(OWN_CAP):
        hit = slot_ref[...] == q
        pick = jnp.where(hit, 1.0, 0.0).astype(bf16)
        picked = jnp.dot(pick, x_ref[...], preferred_element_type=f32)
        for k in range(parts):
            wide_ref[pl.ds(q * parts + k, owners, stride=stride), :] = picked[
                :, k * LANES : (k + 1) * LANES
            ]
        held = jnp.sum(jnp.where(hit, key, 0.0), axis=1, keepdims=True)
        table = jnp.where(lane // 8 == q, held, table)
    table = table.astype(jnp.int32)
    meta = jnp.where(
        lane % 8 == 0,
        table % DIGIT,
        jnp.where(
            lane % 8 == 1,
            table // DIGIT % DIGIT,
            jnp.where(lane % 8 == 2, table // DIGIT**2, 0),
        ),
    ).astype(f32)
    wide_ref[pl.ds(OWN_CAP * parts, owners, stride=stride), :] = meta
    wide_ref[pl.ds(OWN_CAP * parts + 1, owners, stride=stride), :] = jnp.zeros_like(meta)
    w_ref[...] = wide_ref[...].astype(bf16)


def score_kernel(
    label_span, w_ref, out_ref, wide_ref, x_ref, key_ref, label_ref, scale_ref, turned_ref
):
    sources = out_ref.shape[0]
    width = x_ref.shape[1]
    parts = width // LANES
    stride = w_ref.shape[0] // sources
    minus = -jnp.inf
    wide_ref[...] = w_ref[...].astype(f32)
    meta = wide_ref[pl.ds(OWN_CAP * parts, sources, stride=stride), :]
    lane = iota((sources, LANES), 1)
    table = jnp.zeros((sources, LANES), f32)
    for r in range(OWN_CAP):
        own = slice(r * sources, (r + 1) * sources)
        key = (
            meta[:, 8 * r : 8 * r + 1]
            + DIGIT * meta[:, 8 * r + 1 : 8 * r + 2]
            + DIGIT**2 * meta[:, 8 * r + 2 : 8 * r + 3]
        )
        label = jnp.where(key > label_span, 1.0, jnp.where(key > 0, 0.0, 2.0))
        key_ref[own, :] = jnp.broadcast_to(key, (sources, LANES))
        label_ref[own, :] = jnp.broadcast_to(label, (sources, LANES))
        table = jnp.where(lane == r, key, jnp.where(lane == r + 8, label, table))
    turned_ref[...] = table.T
    here = iota((sources, sources), 0) == iota((sources, sources), 1)
    result = jnp.full((sources, LANES), -1.0, f32)
    tops = jnp.full((8, sources), -1.0, f32)
    halves = sources // LANES
    second = [[jnp.full((8, LANES), minus, f32)] * halves for _ in range(OWN_CAP)]
    for r in range(OWN_CAP):
        own = slice(r * sources, (r + 1) * sources)
        for k in range(parts):
            x_ref[own, k * LANES : (k + 1) * LANES] = wide_ref[
                pl.ds(r * parts + k, sources, stride=stride), :
            ].astype(bf16)
        first = [jnp.full((STEP, LANES), minus, f32)] * (sources // STEP)
        for t in [r, *range(r)]:
            scores = lax.dot_general(
                x_ref[own, :],
                x_ref[t * sources : (t + 1) * sources, :],
                (((1,), (1,)), ((), ())),
                preferred_element_type=f32,
            )
            if t == r:
                squares = jnp.where(here, scores, 0.0)
                scale = lax.rsqrt(jnp.sum(squares, axis=1, keepdims=True) + norm_eps)
                scale_ref[own, :] = jnp.broadcast_to(scale, (sources, LANES))
                turned_ref[16 + r : 17 + r, :] = lax.rsqrt(
                    jnp.sum(squares, axis=0, keepdims=True) + norm_eps
                )
            for i in range(sources // STEP):
                rows = slice(i * STEP, (i + 1) * STEP)
                at = slice(r * sources + i * STEP, r * sources + (i + 1) * STEP)
                for h in range(halves):
                    cols = slice(h * LANES, (h + 1) * LANES)
                    like = label_ref[at, :] == turned_ref[8 + t : 9 + t, cols]
                    score = jnp.where(like, scores[rows, cols], minus)
                    later = turned_ref[t : t + 1, cols] < key_ref[at, :]
                    forward = jnp.where(later, score * turned_ref[16 + t : 17 + t, cols], minus)
                    first[i] = jnp.maximum(first[i], forward)
                    if t != r:
                        back = jnp.where(later, minus, score * scale_ref[at, :])
                        back = jnp.max(back.reshape(STEP // 8, 8, LANES), axis=0)
                        second[t][h] = jnp.maximum(second[t][h], back)
        top = jnp.concatenate([jnp.max(f, axis=1, keepdims=True) for f in first], axis=0)
        result = jnp.where(lane == r, top * scale_ref[own, :], result)
    for t in range(OWN_CAP):
        top = jnp.concatenate([jnp.max(s, axis=0, keepdims=True) for s in second[t]], axis=1)
        top = top * turned_ref[16 + t : 17 + t, :]
        tops = jnp.where(iota((8, sources), 0) == t, top, tops)
    turned_ref[:8, :] = tops
    result = jnp.maximum(jnp.maximum(result, turned_ref[...].T), -1.0)
    out_ref[...] = result[:, :OWN_CAP]


def pick_kernel(r_ref, slot_ref, out_ref):
    slot = slot_ref[...]
    value = jnp.zeros(slot.shape, f32)
    for q in range(OWN_CAP):
        value = jnp.where(slot == q, r_ref[:, q : q + 1], value)
    out_ref[...] = jnp.sum(value, axis=0, keepdims=True)


def call(kernel, out_shape, scratch, name, **rest):
    return pl.pallas_call(
        kernel,
        out_shape=out_shape,
        scratch_shapes=scratch,
        compiler_params=pltpu.CompilerParams(vmem_limit_bytes=48 * 2**20),
        name=name,
        **rest,
    )


def stay(value):
    return pltpu.with_memory_space_constraint(value, pltpu.HBM)


def shards(embeddings, clusters, priorities):
    rows, width = embeddings.shape
    owners = lax.axis_size("gx") * lax.axis_size("gy")
    label_span = rows * owners
    height = owners * (OWN_CAP * width // LANES + META)
    slots = owners * OWN_CAP
    wide = pltpu.VMEM((height, LANES), f32)
    packed, slot = call(
        functools.partial(pack_kernel, label_span),
        (
            jax.ShapeDtypeStruct((height, LANES), bf16),
            jax.ShapeDtypeStruct((owners, rows), f32),
        ),
        [
            wide,
            pltpu.VMEM((1, rows), jnp.int32),
            pltpu.VMEM((1, rows), jnp.int32),
            pltpu.VMEM((rows, width), bf16),
            pltpu.SemaphoreType.DMA((2 + X_PIECES,)),
        ],
        "pack",
        in_specs=[pl.BlockSpec(memory_space=pltpu.HBM)] * 3,
    )(stay(clusters.reshape(1, rows)), stay(priorities.reshape(1, rows)), stay(embeddings))
    arrived = lax.all_to_all(
        packed.reshape(owners, height // owners // 2, 2, LANES),
        ("gx", "gy"),
        split_axis=0,
        concat_axis=0,
        tiled=True,
    ).reshape(height, LANES)
    result = call(
        functools.partial(score_kernel, label_span),
        jax.ShapeDtypeStruct((owners, OWN_CAP), f32),
        [
            wide,
            pltpu.VMEM((slots, width), bf16),
            pltpu.VMEM((slots, LANES), f32),
            pltpu.VMEM((slots, LANES), f32),
            pltpu.VMEM((slots, LANES), f32),
            pltpu.VMEM((LANES, owners), f32),
        ],
        "score",
    )(arrived)
    returned = lax.all_to_all(result, ("gx", "gy"), split_axis=0, concat_axis=0, tiled=True)
    best = call(pick_kernel, jax.ShapeDtypeStruct((1, rows), f32), [], "pick")(returned, slot)
    return best.reshape(rows)


def solution(mesh):
    in_specs = (P(("gx", "gy"), None), P(("gx", "gy")), P(("gx", "gy")))
    out_specs = P(("gx", "gy"))
    return jax.shard_map(shards, mesh=mesh, in_specs=in_specs, out_specs=out_specs, check_vma=False)
```

```python
import functools

import jax
import jax.numpy as jnp
from jax import lax
from jax.experimental import pallas as pl
from jax.experimental.pallas import tpu as pltpu
from jax.sharding import PartitionSpec as P

CLUS_DEV = 2
OWN_CAP = 6
LANES = 128
META = 2
DIGIT = 128
X_PIECES = 1
WIDE = 256

norm_eps = 1e-06
bf16 = jnp.bfloat16
f32 = jnp.float32


def iota(shape, dim):
    return lax.broadcasted_iota(jnp.int32, shape, dim)


def pack_kernel(
    label_span, c_hbm, p_hbm, x_hbm, w_ref, slot_ref, wide_ref, c_ref, p_ref, x_ref, sems, pick_ref
):
    owners, rows = slot_ref.shape
    width = x_ref.shape[1]
    parts = width // LANES
    stride = w_ref.shape[0] // owners
    block = min(256, rows)
    copies = [
        pltpu.make_async_copy(c_hbm, c_ref, sems.at[0]),
        pltpu.make_async_copy(p_hbm, p_ref, sems.at[1]),
    ]
    piece = rows // X_PIECES
    for i in range(X_PIECES):
        span = pl.ds(i * piece, piece)
        copies.append(pltpu.make_async_copy(x_hbm.at[span], x_ref.at[span], sems.at[2 + i]))
    for copy in copies:
        copy.start()
    before = (iota((block, block), 0) < iota((block, block), 1)).astype(f32).astype(bf16)
    copies[0].wait()
    copies[1].wait()
    clusters = c_ref[...]
    owner = clusters // CLUS_DEV
    key = (clusters % CLUS_DEV) * label_span + p_ref[...] + 1
    ones = jnp.ones((block, block), bf16)
    earlier = None
    for b in range(rows // block):
        cols = slice(b * block, (b + 1) * block)
        named = iota((owners, block), 0) == owner[:, cols]
        count = named.astype(f32).astype(bf16)
        rank = jnp.dot(count, before, preferred_element_type=f32)
        if b:
            rank = rank + jnp.dot(earlier, ones, preferred_element_type=f32)
        earlier = earlier + count if b else count
        slot_ref[:, cols] = jnp.where(named, rank, -1.0)
    key = key.astype(f32)
    lane = iota((owners, LANES), 1)
    table = jnp.zeros((owners, LANES), f32)
    for q in range(OWN_CAP):
        hit = slot_ref[...] == q
        pick_ref[q * owners : (q + 1) * owners, :] = jnp.where(hit, 1.0, 0.0).astype(bf16)
        held = jnp.sum(jnp.where(hit, key, 0.0), axis=1, keepdims=True)
        table = jnp.where(lane // 8 == q, held, table)
    for copy in copies[2:]:
        copy.wait()
    for n in range(width // WIDE):
        picked = jnp.dot(
            pick_ref[...], x_ref[:, n * WIDE : (n + 1) * WIDE], preferred_element_type=f32
        )
        for q in range(OWN_CAP):
            for h in range(WIDE // LANES):
                at = q * parts + n * (WIDE // LANES) + h
                wide_ref[pl.ds(at, owners, stride=stride), :] = picked[
                    q * owners : (q + 1) * owners, h * LANES : (h + 1) * LANES
                ]
    table = table.astype(jnp.int32)
    meta = jnp.where(
        lane % 8 == 0,
        table % DIGIT,
        jnp.where(
            lane % 8 == 1,
            table // DIGIT % DIGIT,
            jnp.where(lane % 8 == 2, table // DIGIT**2, 0),
        ),
    ).astype(f32)
    wide_ref[pl.ds(OWN_CAP * parts, owners, stride=stride), :] = meta
    wide_ref[pl.ds(OWN_CAP * parts + 1, owners, stride=stride), :] = jnp.zeros_like(meta)
    w_ref[...] = wide_ref[...].astype(bf16)


def score_kernel(
    label_span, w_ref, out_ref, wide_ref, x_ref, key_ref, label_ref, scale_ref, turned_ref, tile_ref, first_ref
):
    sources = out_ref.shape[0]
    width = x_ref.shape[1]
    parts = width // LANES
    stride = w_ref.shape[0] // sources
    minus = -jnp.inf
    wide_ref[...] = w_ref[...].astype(f32)
    meta = wide_ref[pl.ds(OWN_CAP * parts, sources, stride=stride), :]
    lane = iota((sources, LANES), 1)
    table = jnp.zeros((sources, LANES), f32)
    for r in range(OWN_CAP):
        own = slice(r * sources, (r + 1) * sources)
        key = (
            meta[:, 8 * r : 8 * r + 1]
            + DIGIT * meta[:, 8 * r + 1 : 8 * r + 2]
            + DIGIT**2 * meta[:, 8 * r + 2 : 8 * r + 3]
        )
        label = jnp.where(key > label_span, 1.0, jnp.where(key > 0, 0.0, 2.0))
        key_ref[own, :] = jnp.broadcast_to(key, (sources, LANES))
        label_ref[own, :] = jnp.broadcast_to(label, (sources, LANES))
        table = jnp.where(lane == r, key, jnp.where(lane == r + 8, label, table))
    turned_ref[...] = table.T
    here = iota((sources, sources), 0) == iota((sources, sources), 1)
    result = jnp.full((sources, LANES), -1.0, f32)
    tops = jnp.full((8, sources), -1.0, f32)
    halves = sources // LANES
    second = [[jnp.full((8, LANES), minus, f32)] * halves for _ in range(OWN_CAP)]
    first = {}
    tiles = [(r, t) for r in range(OWN_CAP) for t in [r, *range(r)]]
    for m, (r, t) in enumerate(tiles):
        own = slice(r * sources, (r + 1) * sources)
        if t == r:
            for k in range(parts):
                x_ref[own, k * LANES : (k + 1) * LANES] = wide_ref[
                    pl.ds(r * parts + k, sources, stride=stride), :
                ].astype(bf16)
        tile_ref[m] = lax.dot_general(
            x_ref[own, :],
            x_ref[t * sources : (t + 1) * sources, :],
            (((1,), (1,)), ((), ())),
            preferred_element_type=f32,
        )
        if t == r:
            squares = jnp.where(here, tile_ref[m], 0.0)
            scale = lax.rsqrt(jnp.sum(squares, axis=1, keepdims=True) + norm_eps)
            scale_ref[own, :] = jnp.broadcast_to(scale, (sources, LANES))
            turned_ref[16 + r : 17 + r, :] = lax.rsqrt(
                jnp.sum(squares, axis=0, keepdims=True) + norm_eps
            )
        spans = [slice(h * LANES, (h + 1) * LANES) for h in range(halves)]
        label_row = [jnp.broadcast_to(turned_ref[8 + t : 9 + t, c], (8, LANES)) for c in spans]
        key_row = [jnp.broadcast_to(turned_ref[t : t + 1, c], (8, LANES)) for c in spans]
        scale_row = [jnp.broadcast_to(turned_ref[16 + t : 17 + t, c], (8, LANES)) for c in spans]
        for i in range(sources // 8):
            at = slice(r * sources + i * 8, r * sources + i * 8 + 8)
            label_col, key_col = label_ref[at, :], key_ref[at, :]
            if t != r:
                scale_col = scale_ref[at, :]
            forwards = []
            for h in range(halves):
                score = tile_ref[m, i * 8 : (i + 1) * 8, spans[h]]
                score = jnp.where(label_col == label_row[h], score, minus)
                later = key_row[h] < key_col
                forward = jnp.where(later, score * scale_row[h], minus)
                forwards.append(forward)
                if t != r:
                    back = jnp.where(later, minus, score * scale_col)
                    second[t][h] = jnp.maximum(second[t][h], back)
            best = jnp.maximum(*forwards)
            first_ref[i * 8 : i * 8 + 8, :] = best if t == r else jnp.maximum(first_ref[i * 8 : i * 8 + 8, :], best)
        if m + 1 == len(tiles) or tiles[m + 1][0] != r:
            top = jnp.max(first_ref[...], axis=1, keepdims=True)
            result = jnp.where(lane == r, top * scale_ref[own, :], result)
    for t in range(OWN_CAP):
        top = jnp.concatenate([jnp.max(s, axis=0, keepdims=True) for s in second[t]], axis=1)
        top = top * turned_ref[16 + t : 17 + t, :]
        tops = jnp.where(iota((8, sources), 0) == t, top, tops)
    turned_ref[:8, :] = tops
    result = jnp.maximum(jnp.maximum(result, turned_ref[...].T), -1.0)
    out_ref[...] = result[:, :OWN_CAP]


def pick_kernel(r_ref, slot_ref, out_ref):
    slot = slot_ref[...]
    value = jnp.zeros(slot.shape, f32)
    for q in range(OWN_CAP):
        value = jnp.where(slot == q, r_ref[:, q : q + 1], value)
    out_ref[...] = jnp.sum(value, axis=0, keepdims=True)


def call(kernel, out_shape, scratch, name, **rest):
    return pl.pallas_call(
        kernel,
        out_shape=out_shape,
        scratch_shapes=scratch,
        compiler_params=pltpu.CompilerParams(vmem_limit_bytes=48 * 2**20),
        name=name,
        **rest,
    )


def stay(value):
    return pltpu.with_memory_space_constraint(value, pltpu.HBM)


def shards(embeddings, clusters, priorities):
    rows, width = embeddings.shape
    owners = lax.axis_size("gx") * lax.axis_size("gy")
    label_span = rows * owners
    height = owners * (OWN_CAP * width // LANES + META)
    slots = owners * OWN_CAP
    wide = pltpu.VMEM((height, LANES), f32)
    packed, slot = call(
        functools.partial(pack_kernel, label_span),
        (
            jax.ShapeDtypeStruct((height, LANES), bf16),
            jax.ShapeDtypeStruct((owners, rows), f32),
        ),
        [
            wide,
            pltpu.VMEM((1, rows), jnp.int32),
            pltpu.VMEM((1, rows), jnp.int32),
            pltpu.VMEM((rows, width), bf16),
            pltpu.SemaphoreType.DMA((2 + X_PIECES,)),
            pltpu.VMEM((slots, rows), bf16),
        ],
        "pack",
        in_specs=[pl.BlockSpec(memory_space=pltpu.HBM)] * 3,
    )(stay(clusters.reshape(1, rows)), stay(priorities.reshape(1, rows)), stay(embeddings))
    arrived = lax.all_to_all(
        packed.reshape(owners, height // owners // 2, 2, LANES),
        ("gx", "gy"),
        split_axis=0,
        concat_axis=0,
        tiled=True,
    ).reshape(height, LANES)
    result = call(
        functools.partial(score_kernel, label_span),
        jax.ShapeDtypeStruct((owners, OWN_CAP), f32),
        [
            wide,
            pltpu.VMEM((slots, width), bf16),
            pltpu.VMEM((slots, LANES), f32),
            pltpu.VMEM((slots, LANES), f32),
            pltpu.VMEM((slots, LANES), f32),
            pltpu.VMEM((LANES, owners), f32),
            pltpu.VMEM((OWN_CAP * (OWN_CAP + 1) // 2, owners, owners), f32),
            pltpu.VMEM((owners, LANES), f32),
        ],
        "score",
    )(arrived)
    returned = lax.all_to_all(result, ("gx", "gy"), split_axis=0, concat_axis=0, tiled=True)
    best = call(pick_kernel, jax.ShapeDtypeStruct((1, rows), f32), [], "pick")(returned, slot)
    return best.reshape(rows)


def solution(mesh):
    in_specs = (P(("gx", "gy"), None), P(("gx", "gy")), P(("gx", "gy")))
    out_specs = P(("gx", "gy"))
    return jax.shard_map(shards, mesh=mesh, in_specs=in_specs, out_specs=out_specs, check_vma=False)
```

```python
import functools

import jax
import jax.numpy as jnp
from jax import lax
from jax.experimental import pallas as pl
from jax.experimental.pallas import tpu as pltpu
from jax.sharding import PartitionSpec as P

CLUS_DEV = 2
OWN_CAP = 6
LANES = 128
META = 2
DIGIT = 128
X_PIECES = 1
GROUPS = 2

norm_eps = 1e-06
bf16 = jnp.bfloat16
f32 = jnp.float32


def iota(shape, dim):
    return lax.broadcasted_iota(jnp.int32, shape, dim)


def pack_kernel(
    label_span,
    c_hbm,
    p_hbm,
    x_hbm,
    w_ref,
    named_ref,
    rank_ref,
    wide_ref,
    c_ref,
    p_ref,
    x_ref,
    sems,
    pick_ref,
    slot_ref,
):
    owners, rows = slot_ref.shape
    width = x_ref.shape[1]
    parts = width // LANES
    stride = w_ref.shape[0] // owners
    block = min(256, rows)
    copies = [
        pltpu.make_async_copy(c_hbm, c_ref, sems.at[0]),
        pltpu.make_async_copy(p_hbm, p_ref, sems.at[1]),
    ]
    piece = rows // X_PIECES
    for i in range(X_PIECES):
        span = pl.ds(i * piece, piece)
        copies.append(pltpu.make_async_copy(x_hbm.at[span], x_ref.at[span], sems.at[2 + i]))
    for copy in copies:
        copy.start()
    before = (iota((block, block), 0) < iota((block, block), 1)).astype(f32).astype(bf16)
    copies[0].wait()
    copies[1].wait()
    clusters = c_ref[...]
    owner = clusters // CLUS_DEV
    key = (clusters % CLUS_DEV) * label_span + p_ref[...] + 1
    ones = jnp.ones((block, block), bf16)
    earlier = None
    for b in range(rows // block):
        cols = slice(b * block, (b + 1) * block)
        named = iota((owners, block), 0) == owner[:, cols]
        count = named.astype(f32).astype(bf16)
        rank = jnp.dot(count, before, preferred_element_type=f32)
        if b:
            rank = rank + jnp.dot(earlier, ones, preferred_element_type=f32)
        earlier = earlier + count if b else count
        slot_ref[:, cols] = jnp.where(named, rank, -1.0)
        named_ref[:, cols] = count
        rank_ref[:, cols] = jnp.sum(jnp.where(named, rank, 0.0), axis=0, keepdims=True).astype(jnp.int32)
    key = key.astype(f32)
    lane = iota((owners, LANES), 1)
    for copy in copies[2:]:
        copy.wait()
    group = owners // GROUPS
    for g in range(GROUPS):
        some = slice(g * group, (g + 1) * group)
        for q in range(OWN_CAP):
            hit = slot_ref[some, :] == q
            at = (g * OWN_CAP + q) * group
            pick_ref[at : at + group, :] = jnp.where(hit, 1.0, 0.0).astype(bf16)
            held = jnp.sum(jnp.where(hit, key, 0.0), axis=1, keepdims=True)
            table_g = jnp.where(lane[some] // 8 == q, held, 0.0 if q == 0 else table_g)
        picked = jnp.dot(
            pick_ref[g * OWN_CAP * group : (g + 1) * OWN_CAP * group, :],
            x_ref[...],
            preferred_element_type=f32,
        )
        for q in range(OWN_CAP):
            for k in range(parts):
                wide_ref[pl.ds(g * group * stride + q * parts + k, group, stride=stride), :] = picked[
                    q * group : (q + 1) * group, k * LANES : (k + 1) * LANES
                ]
        table_g = table_g.astype(jnp.int32)
        kind = lane[some] % 8
        meta = jnp.where(
            kind == 0,
            table_g % DIGIT,
            jnp.where(
                kind == 1,
                table_g // DIGIT % DIGIT,
                jnp.where(kind == 2, table_g // DIGIT**2, 0),
            ),
        ).astype(f32)
        at = g * group * stride + OWN_CAP * parts
        wide_ref[pl.ds(at, group, stride=stride), :] = meta
        wide_ref[pl.ds(at + 1, group, stride=stride), :] = jnp.zeros_like(meta)
        whole = slice(g * group * stride, (g + 1) * group * stride)
        w_ref[whole, :] = wide_ref[whole, :].astype(bf16)


def score_kernel(
    label_span,
    w_ref,
    out_ref,
    wide_ref,
    x_ref,
    key_ref,
    label_ref,
    scale_ref,
    turned_ref,
    tile_ref,
    first_ref,
):
    sources = out_ref.shape[0]
    width = x_ref.shape[1]
    parts = width // LANES
    stride = w_ref.shape[0] // sources
    minus = -jnp.inf
    wide_ref[...] = w_ref[...].astype(f32)
    meta = wide_ref[pl.ds(OWN_CAP * parts, sources, stride=stride), :]
    lane = iota((sources, LANES), 1)
    table = jnp.zeros((sources, LANES), f32)
    for r in range(OWN_CAP):
        own = slice(r * sources, (r + 1) * sources)
        key = (
            meta[:, 8 * r : 8 * r + 1]
            + DIGIT * meta[:, 8 * r + 1 : 8 * r + 2]
            + DIGIT**2 * meta[:, 8 * r + 2 : 8 * r + 3]
        )
        label = jnp.where(key > label_span, 1.0, jnp.where(key > 0, 0.0, 2.0))
        key_ref[own, :] = jnp.broadcast_to(key, (sources, LANES))
        label_ref[own, :] = jnp.broadcast_to(label, (sources, LANES))
        table = jnp.where(lane == r, key, jnp.where(lane == r + 8, label, table))
    turned_ref[...] = table.T
    here = iota((sources, sources), 0) == iota((sources, sources), 1)
    result = jnp.full((sources, LANES), -1.0, f32)
    tops = jnp.full((8, sources), -1.0, f32)
    halves = sources // LANES
    second = [[jnp.full((8, LANES), minus, f32)] * halves for _ in range(OWN_CAP)]
    first = {}
    tiles = [(r, t) for r in range(OWN_CAP) for t in [r, *range(r)]]
    for m, (r, t) in enumerate(tiles):
        own = slice(r * sources, (r + 1) * sources)
        if t == r:
            for k in range(parts):
                x_ref[own, k * LANES : (k + 1) * LANES] = wide_ref[
                    pl.ds(r * parts + k, sources, stride=stride), :
                ].astype(bf16)
        tile_ref[m] = lax.dot_general(
            x_ref[own, :],
            x_ref[t * sources : (t + 1) * sources, :],
            (((1,), (1,)), ((), ())),
            preferred_element_type=f32,
        )
        if t == r:
            squares = jnp.where(here, tile_ref[m], 0.0)
            scale = lax.rsqrt(jnp.sum(squares, axis=1, keepdims=True) + norm_eps)
            scale_ref[own, :] = jnp.broadcast_to(scale, (sources, LANES))
            turned_ref[16 + r : 17 + r, :] = lax.rsqrt(
                jnp.sum(squares, axis=0, keepdims=True) + norm_eps
            )
        spans = [slice(h * LANES, (h + 1) * LANES) for h in range(halves)]
        label_row = [jnp.broadcast_to(turned_ref[8 + t : 9 + t, c], (8, LANES)) for c in spans]
        key_row = [jnp.broadcast_to(turned_ref[t : t + 1, c], (8, LANES)) for c in spans]
        scale_row = [jnp.broadcast_to(turned_ref[16 + t : 17 + t, c], (8, LANES)) for c in spans]
        for i in range(sources // 8):
            at = slice(r * sources + i * 8, r * sources + i * 8 + 8)
            label_col, key_col = label_ref[at, :], key_ref[at, :]
            if t != r:
                scale_col = scale_ref[at, :]
            forwards = []
            for h in range(halves):
                score = tile_ref[m, i * 8 : (i + 1) * 8, spans[h]]
                score = jnp.where(label_col == label_row[h], score, minus)
                later = key_row[h] < key_col
                forward = jnp.where(later, score * scale_row[h], minus)
                forwards.append(forward)
                if t != r:
                    back = jnp.where(later, minus, score * scale_col)
                    second[t][h] = jnp.maximum(second[t][h], back)
            best = jnp.maximum(*forwards)
            eight = slice(i * 8, i * 8 + 8)
            first_ref[eight, :] = best if t == r else jnp.maximum(first_ref[eight, :], best)
        if m + 1 == len(tiles) or tiles[m + 1][0] != r:
            top = jnp.max(first_ref[...], axis=1, keepdims=True)
            result = jnp.where(lane == r, top * scale_ref[own, :], result)
    for t in range(OWN_CAP):
        top = jnp.concatenate([jnp.max(s, axis=0, keepdims=True) for s in second[t]], axis=1)
        top = top * turned_ref[16 + t : 17 + t, :]
        tops = jnp.where(iota((8, sources), 0) == t, top, tops)
    turned_ref[:8, :] = tops
    result = jnp.maximum(jnp.maximum(result, turned_ref[...].T), -1.0)
    out_ref[...] = result[:, :OWN_CAP]


def pick_kernel(r_ref, named_ref, rank_ref, out_ref):
    owners, rows = named_ref.shape
    padded = jnp.concatenate([r_ref[...], jnp.zeros((owners, LANES - r_ref.shape[1]), f32)], axis=1)
    rest = padded.T[:8, :]
    pieces = []
    for _ in range(3):
        pieces.append(rest.astype(bf16).astype(f32))
        rest = rest - pieces[-1]
    found = jnp.dot(
        jnp.concatenate(pieces, axis=0).astype(bf16), named_ref[...], preferred_element_type=f32
    )
    value = found[:8] + found[8:16] + found[16:]
    value = jnp.where(iota((8, rows), 0) == rank_ref[...], value, 0.0)
    out_ref[...] = jnp.sum(value, axis=0, keepdims=True)


def call(kernel, out_shape, scratch, name, **rest):
    return pl.pallas_call(
        kernel,
        out_shape=out_shape,
        scratch_shapes=scratch,
        compiler_params=pltpu.CompilerParams(vmem_limit_bytes=48 * 2**20),
        name=name,
        **rest,
    )


def stay(value):
    return pltpu.with_memory_space_constraint(value, pltpu.HBM)


def shards(embeddings, clusters, priorities):
    rows, width = embeddings.shape
    owners = lax.axis_size("gx") * lax.axis_size("gy")
    label_span = rows * owners
    height = owners * (OWN_CAP * width // LANES + META)
    slots = owners * OWN_CAP
    wide = pltpu.VMEM((height, LANES), f32)
    packed, named, rank = call(
        functools.partial(pack_kernel, label_span),
        (
            jax.ShapeDtypeStruct((height, LANES), bf16),
            jax.ShapeDtypeStruct((owners, rows), bf16),
            jax.ShapeDtypeStruct((1, rows), jnp.int32),
        ),
        [
            wide,
            pltpu.VMEM((1, rows), jnp.int32),
            pltpu.VMEM((1, rows), jnp.int32),
            pltpu.VMEM((rows, width), bf16),
            pltpu.SemaphoreType.DMA((2 + X_PIECES,)),
            pltpu.VMEM((slots, rows), bf16),
            pltpu.VMEM((owners, rows), f32),
        ],
        "pack",
        in_specs=[pl.BlockSpec(memory_space=pltpu.HBM)] * 3,
    )(stay(clusters.reshape(1, rows)), stay(priorities.reshape(1, rows)), stay(embeddings))
    arrived = lax.all_to_all(
        packed.reshape(owners, height // owners // 2, 2, LANES),
        ("gx", "gy"),
        split_axis=0,
        concat_axis=0,
        tiled=True,
    ).reshape(height, LANES)
    result = call(
        functools.partial(score_kernel, label_span),
        jax.ShapeDtypeStruct((owners, OWN_CAP), f32),
        [
            wide,
            pltpu.VMEM((slots, width), bf16),
            pltpu.VMEM((slots, LANES), f32),
            pltpu.VMEM((slots, LANES), f32),
            pltpu.VMEM((slots, LANES), f32),
            pltpu.VMEM((LANES, owners), f32),
            pltpu.VMEM((OWN_CAP * (OWN_CAP + 1) // 2, owners, owners), f32),
            pltpu.VMEM((owners, LANES), f32),
        ],
        "score",
    )(arrived)
    returned = lax.all_to_all(result, ("gx", "gy"), split_axis=0, concat_axis=0, tiled=True)
    best = call(pick_kernel, jax.ShapeDtypeStruct((1, rows), f32), [], "pick")(returned, named, rank)
    return best.reshape(rows)


def solution(mesh):
    in_specs = (P(("gx", "gy"), None), P(("gx", "gy")), P(("gx", "gy")))
    out_specs = P(("gx", "gy"))
    return jax.shard_map(shards, mesh=mesh, in_specs=in_specs, out_specs=out_specs, check_vma=False)
```

```python
import functools

import jax
import jax.numpy as jnp
from jax import lax
from jax.experimental import pallas as pl
from jax.experimental.pallas import tpu as pltpu
from jax.sharding import PartitionSpec as P

CLUS_DEV = 2
OWN_CAP = 6
LANES = 128
META = 2
DIGIT = 128
X_PIECES = 1
GROUPS = 2

norm_eps = 1e-06
bf16 = jnp.bfloat16
f32 = jnp.float32


def iota(shape, dim):
    return lax.broadcasted_iota(jnp.int32, shape, dim)


def pack_kernel(
    label_span,
    c_hbm,
    p_hbm,
    x_hbm,
    w_ref,
    named_ref,
    rank_ref,
    wide_ref,
    c_ref,
    p_ref,
    x_ref,
    sems,
    pick_ref,
    slot_ref,
):
    owners, rows = slot_ref.shape
    width = x_ref.shape[1]
    parts = width // LANES
    stride = w_ref.shape[0] // owners
    block = min(512, rows)
    copies = [
        pltpu.make_async_copy(c_hbm, c_ref, sems.at[0]),
        pltpu.make_async_copy(p_hbm, p_ref, sems.at[1]),
    ]
    piece = rows // X_PIECES
    for i in range(X_PIECES):
        span = pl.ds(i * piece, piece)
        copies.append(pltpu.make_async_copy(x_hbm.at[span], x_ref.at[span], sems.at[2 + i]))
    for copy in copies:
        copy.start()
    before = (iota((block, block), 0) < iota((block, block), 1)).astype(f32).astype(bf16)
    copies[0].wait()
    copies[1].wait()
    clusters = c_ref[...]
    owner = clusters // CLUS_DEV
    key = (clusters % CLUS_DEV) * label_span + p_ref[...] + 1
    carry = jnp.zeros((owners, 1), f32)
    for b in range(rows // block):
        cols = slice(b * block, (b + 1) * block)
        named = iota((owners, block), 0) == owner[:, cols]
        count = named.astype(f32)
        rank = jnp.dot(count.astype(bf16), before, preferred_element_type=f32) + carry
        carry = carry + jnp.sum(count, axis=1, keepdims=True)
        slot_ref[:, cols] = jnp.where(named, rank, -1.0)
        named_ref[:, cols] = count.astype(bf16)
        place = jnp.sum(jnp.where(named, rank, 0.0), axis=0, keepdims=True)
        rank_ref[:, cols] = place.astype(jnp.int32)
    key = key.astype(f32)
    lane = iota((owners, LANES), 1)
    for copy in copies[2:]:
        copy.wait()
    group = owners // GROUPS
    for g in range(GROUPS):
        some = slice(g * group, (g + 1) * group)
        for q in range(OWN_CAP):
            hit = slot_ref[some, :] == q
            at = (g * OWN_CAP + q) * group
            pick_ref[at : at + group, :] = jnp.where(hit, 1.0, 0.0).astype(bf16)
            held = jnp.sum(jnp.where(hit, key, 0.0), axis=1, keepdims=True)
            table_g = jnp.where(lane[some] // 8 == q, held, 0.0 if q == 0 else table_g)
        picked = jnp.dot(
            pick_ref[g * OWN_CAP * group : (g + 1) * OWN_CAP * group, :],
            x_ref[...],
            preferred_element_type=f32,
        )
        for q in range(OWN_CAP):
            for k in range(parts):
                wide_ref[pl.ds(g * group * stride + q * parts + k, group, stride=stride), :] = picked[
                    q * group : (q + 1) * group, k * LANES : (k + 1) * LANES
                ]
        table_g = table_g.astype(jnp.int32)
        kind = lane[some] % 8
        meta = jnp.where(
            kind == 0,
            table_g % DIGIT,
            jnp.where(
                kind == 1,
                table_g // DIGIT % DIGIT,
                jnp.where(kind == 2, table_g // DIGIT**2, 0),
            ),
        ).astype(f32)
        at = g * group * stride + OWN_CAP * parts
        wide_ref[pl.ds(at, group, stride=stride), :] = meta
        wide_ref[pl.ds(at + 1, group, stride=stride), :] = jnp.zeros_like(meta)
        whole = slice(g * group * stride, (g + 1) * group * stride)
        w_ref[whole, :] = wide_ref[whole, :].astype(bf16)


def score_kernel(
    label_span,
    w_ref,
    out_ref,
    wide_ref,
    x_ref,
    key_ref,
    label_ref,
    scale_ref,
    turned_ref,
    tile_ref,
    first_ref,
):
    sources = out_ref.shape[0]
    width = x_ref.shape[1]
    parts = width // LANES
    stride = w_ref.shape[0] // sources
    minus = -jnp.inf
    wide_ref[...] = w_ref[...].astype(f32)
    meta = wide_ref[pl.ds(OWN_CAP * parts, sources, stride=stride), :]
    lane = iota((sources, LANES), 1)
    table = jnp.zeros((sources, LANES), f32)
    for r in range(OWN_CAP):
        own = slice(r * sources, (r + 1) * sources)
        key = (
            meta[:, 8 * r : 8 * r + 1]
            + DIGIT * meta[:, 8 * r + 1 : 8 * r + 2]
            + DIGIT**2 * meta[:, 8 * r + 2 : 8 * r + 3]
        )
        label = jnp.where(key > label_span, 1.0, jnp.where(key > 0, 0.0, 2.0))
        key_ref[own, :] = jnp.broadcast_to(key, (sources, LANES))
        label_ref[own, :] = jnp.broadcast_to(label, (sources, LANES))
        table = jnp.where(lane == r, key, jnp.where(lane == r + 8, label, table))
    turned_ref[...] = table.T
    here = iota((sources, sources), 0) == iota((sources, sources), 1)
    result = jnp.full((sources, LANES), -1.0, f32)
    tops = jnp.full((8, sources), -1.0, f32)
    halves = sources // LANES
    second = [[jnp.full((8, LANES), minus, f32)] * halves for _ in range(OWN_CAP)]
    first = {}
    tiles = [(r, t) for r in range(OWN_CAP) for t in [r, *range(r)]]
    for m, (r, t) in enumerate(tiles):
        own = slice(r * sources, (r + 1) * sources)
        if t == r:
            for k in range(parts):
                x_ref[own, k * LANES : (k + 1) * LANES] = wide_ref[
                    pl.ds(r * parts + k, sources, stride=stride), :
                ].astype(bf16)
        tile_ref[m] = lax.dot_general(
            x_ref[own, :],
            x_ref[t * sources : (t + 1) * sources, :],
            (((1,), (1,)), ((), ())),
            preferred_element_type=f32,
        )
        if t == r:
            squares = jnp.where(here, tile_ref[m], 0.0)
            scale = lax.rsqrt(jnp.sum(squares, axis=1, keepdims=True) + norm_eps)
            scale_ref[own, :] = jnp.broadcast_to(scale, (sources, LANES))
            turned_ref[16 + r : 17 + r, :] = lax.rsqrt(
                jnp.sum(squares, axis=0, keepdims=True) + norm_eps
            )
        spans = [slice(h * LANES, (h + 1) * LANES) for h in range(halves)]
        label_row = [jnp.broadcast_to(turned_ref[8 + t : 9 + t, c], (8, LANES)) for c in spans]
        key_row = [jnp.broadcast_to(turned_ref[t : t + 1, c], (8, LANES)) for c in spans]
        scale_row = [jnp.broadcast_to(turned_ref[16 + t : 17 + t, c], (8, LANES)) for c in spans]
        for i in range(sources // 8):
            at = slice(r * sources + i * 8, r * sources + i * 8 + 8)
            label_col, key_col = label_ref[at, :], key_ref[at, :]
            if t != r:
                scale_col = scale_ref[at, :]
            forwards = []
            for h in range(halves):
                score = tile_ref[m, i * 8 : (i + 1) * 8, spans[h]]
                score = jnp.where(label_col == label_row[h], score, minus)
                later = key_row[h] < key_col
                forward = jnp.where(later, score * scale_row[h], minus)
                forwards.append(forward)
                if t != r:
                    back = jnp.where(later, minus, score * scale_col)
                    second[t][h] = jnp.maximum(second[t][h], back)
            best = jnp.maximum(*forwards)
            eight = slice(i * 8, i * 8 + 8)
            first_ref[eight, :] = best if t == r else jnp.maximum(first_ref[eight, :], best)
        if m + 1 == len(tiles) or tiles[m + 1][0] != r:
            top = jnp.max(first_ref[...], axis=1, keepdims=True)
            result = jnp.where(lane == r, top * scale_ref[own, :], result)
    for t in range(OWN_CAP):
        top = jnp.concatenate([jnp.max(s, axis=0, keepdims=True) for s in second[t]], axis=1)
        top = top * turned_ref[16 + t : 17 + t, :]
        tops = jnp.where(iota((8, sources), 0) == t, top, tops)
    turned_ref[:8, :] = tops
    result = jnp.maximum(jnp.maximum(result, turned_ref[...].T), -1.0)
    out_ref[...] = result[:, :OWN_CAP]


def pick_kernel(r_ref, named_ref, rank_ref, out_ref):
    owners, rows = named_ref.shape
    padded = jnp.concatenate([r_ref[...], jnp.zeros((owners, LANES - r_ref.shape[1]), f32)], axis=1)
    rest = padded.T[:8, :]
    pieces = []
    for _ in range(3):
        pieces.append(rest.astype(bf16).astype(f32))
        rest = rest - pieces[-1]
    found = jnp.dot(
        jnp.concatenate(pieces, axis=0).astype(bf16), named_ref[...], preferred_element_type=f32
    )
    value = found[:8] + found[8:16] + found[16:]
    value = jnp.where(iota((8, rows), 0) == rank_ref[...], value, 0.0)
    out_ref[...] = jnp.sum(value, axis=0, keepdims=True)


def call(kernel, out_shape, scratch, name, **rest):
    return pl.pallas_call(
        kernel,
        out_shape=out_shape,
        scratch_shapes=scratch,
        compiler_params=pltpu.CompilerParams(vmem_limit_bytes=48 * 2**20),
        name=name,
        **rest,
    )


def stay(value):
    return pltpu.with_memory_space_constraint(value, pltpu.HBM)


def shards(embeddings, clusters, priorities):
    rows, width = embeddings.shape
    owners = lax.axis_size("gx") * lax.axis_size("gy")
    label_span = rows * owners
    height = owners * (OWN_CAP * width // LANES + META)
    slots = owners * OWN_CAP
    wide = pltpu.VMEM((height, LANES), f32)
    packed, named, rank = call(
        functools.partial(pack_kernel, label_span),
        (
            jax.ShapeDtypeStruct((height, LANES), bf16),
            jax.ShapeDtypeStruct((owners, rows), bf16),
            jax.ShapeDtypeStruct((1, rows), jnp.int32),
        ),
        [
            wide,
            pltpu.VMEM((1, rows), jnp.int32),
            pltpu.VMEM((1, rows), jnp.int32),
            pltpu.VMEM((rows, width), bf16),
            pltpu.SemaphoreType.DMA((2 + X_PIECES,)),
            pltpu.VMEM((slots, rows), bf16),
            pltpu.VMEM((owners, rows), f32),
        ],
        "pack",
        in_specs=[pl.BlockSpec(memory_space=pltpu.HBM)] * 3,
    )(stay(clusters.reshape(1, rows)), stay(priorities.reshape(1, rows)), stay(embeddings))
    arrived = lax.all_to_all(
        packed.reshape(owners, height // owners // 2, 2, LANES),
        ("gx", "gy"),
        split_axis=0,
        concat_axis=0,
        tiled=True,
    ).reshape(height, LANES)
    result = call(
        functools.partial(score_kernel, label_span),
        jax.ShapeDtypeStruct((owners, OWN_CAP), f32),
        [
            wide,
            pltpu.VMEM((slots, width), bf16),
            pltpu.VMEM((slots, LANES), f32),
            pltpu.VMEM((slots, LANES), f32),
            pltpu.VMEM((slots, LANES), f32),
            pltpu.VMEM((LANES, owners), f32),
            pltpu.VMEM((OWN_CAP * (OWN_CAP + 1) // 2, owners, owners), f32),
            pltpu.VMEM((owners, LANES), f32),
        ],
        "score",
    )(arrived)
    returned = lax.all_to_all(result, ("gx", "gy"), split_axis=0, concat_axis=0, tiled=True)
    best = call(pick_kernel, jax.ShapeDtypeStruct((1, rows), f32), [], "pick")(returned, named, rank)
    return best.reshape(rows)


def solution(mesh):
    in_specs = (P(("gx", "gy"), None), P(("gx", "gy")), P(("gx", "gy")))
    out_specs = P(("gx", "gy"))
    return jax.shard_map(shards, mesh=mesh, in_specs=in_specs, out_specs=out_specs, check_vma=False)
```

```python
import functools

import jax
import jax.numpy as jnp
from jax import lax
from jax.experimental import pallas as pl
from jax.experimental.pallas import tpu as pltpu
from jax.sharding import Mesh
from jax.sharding import PartitionSpec as P

CLUS_DEV = 2
OWN_CAP = 6
LANES = 128
AXES = ("z", "x", "core", "gy")
PLACE = (4, 2)
ORDER = ("core", "x", "gy", "z")
META = 2
DIGIT = 128
X_PIECES = 1
GROUPS = 2

norm_eps = 1e-06
bf16 = jnp.bfloat16
f32 = jnp.float32


def iota(shape, dim):
    return lax.broadcasted_iota(jnp.int32, shape, dim)


def pack_kernel(
    label_span,
    c_hbm,
    p_hbm,
    x_hbm,
    w_ref,
    named_ref,
    rank_ref,
    wide_ref,
    c_ref,
    p_ref,
    x_ref,
    sems,
    pick_ref,
    slot_ref,
):
    owners, rows = slot_ref.shape
    width = x_ref.shape[1]
    parts = width // LANES
    stride = w_ref.shape[0] // owners
    block = min(512, rows)
    copies = [
        pltpu.make_async_copy(c_hbm, c_ref, sems.at[0]),
        pltpu.make_async_copy(p_hbm, p_ref, sems.at[1]),
    ]
    piece = rows // X_PIECES
    for i in range(X_PIECES):
        span = pl.ds(i * piece, piece)
        copies.append(pltpu.make_async_copy(x_hbm.at[span], x_ref.at[span], sems.at[2 + i]))
    for copy in copies:
        copy.start()
    before = (iota((block, block), 0) < iota((block, block), 1)).astype(f32).astype(bf16)
    copies[0].wait()
    copies[1].wait()
    clusters = c_ref[...]
    owner = clusters // CLUS_DEV
    key = (clusters % CLUS_DEV) * label_span + p_ref[...] + 1
    carry = jnp.zeros((owners, 1), f32)
    for b in range(rows // block):
        cols = slice(b * block, (b + 1) * block)
        named = iota((owners, block), 0) == owner[:, cols]
        count = named.astype(f32)
        rank = jnp.dot(count.astype(bf16), before, preferred_element_type=f32) + carry
        carry = carry + jnp.sum(count, axis=1, keepdims=True)
        slot_ref[:, cols] = jnp.where(named, rank, -1.0)
        named_ref[:, cols] = count.astype(bf16)
        place = jnp.sum(jnp.where(named, rank, 0.0), axis=0, keepdims=True)
        rank_ref[:, cols] = place.astype(jnp.int32)
    key = key.astype(f32)
    lane = iota((owners, LANES), 1)
    for copy in copies[2:]:
        copy.wait()
    group = owners // GROUPS
    for g in range(GROUPS):
        some = slice(g * group, (g + 1) * group)
        for q in range(OWN_CAP):
            hit = slot_ref[some, :] == q
            at = (g * OWN_CAP + q) * group
            pick_ref[at : at + group, :] = jnp.where(hit, 1.0, 0.0).astype(bf16)
            held = jnp.sum(jnp.where(hit, key, 0.0), axis=1, keepdims=True)
            table_g = jnp.where(lane[some] // 8 == q, held, 0.0 if q == 0 else table_g)
        picked = jnp.dot(
            pick_ref[g * OWN_CAP * group : (g + 1) * OWN_CAP * group, :],
            x_ref[...],
            preferred_element_type=f32,
        )
        for q in range(OWN_CAP):
            for k in range(parts):
                wide_ref[pl.ds(g * group * stride + q * parts + k, group, stride=stride), :] = picked[
                    q * group : (q + 1) * group, k * LANES : (k + 1) * LANES
                ]
        table_g = table_g.astype(jnp.int32)
        kind = lane[some] % 8
        meta = jnp.where(
            kind == 0,
            table_g % DIGIT,
            jnp.where(
                kind == 1,
                table_g // DIGIT % DIGIT,
                jnp.where(kind == 2, table_g // DIGIT**2, 0),
            ),
        ).astype(f32)
        at = g * group * stride + OWN_CAP * parts
        wide_ref[pl.ds(at, group, stride=stride), :] = meta
        wide_ref[pl.ds(at + 1, group, stride=stride), :] = jnp.zeros_like(meta)
        whole = slice(g * group * stride, (g + 1) * group * stride)
        w_ref[whole, :] = wide_ref[whole, :].astype(bf16)


def score_kernel(
    label_span,
    w_ref,
    out_ref,
    wide_ref,
    x_ref,
    key_ref,
    label_ref,
    scale_ref,
    turned_ref,
    tile_ref,
    first_ref,
):
    sources = out_ref.shape[0]
    width = x_ref.shape[1]
    parts = width // LANES
    stride = w_ref.shape[0] // sources
    minus = -jnp.inf
    wide_ref[...] = w_ref[...].astype(f32)
    meta = wide_ref[pl.ds(OWN_CAP * parts, sources, stride=stride), :]
    lane = iota((sources, LANES), 1)
    table = jnp.zeros((sources, LANES), f32)
    for r in range(OWN_CAP):
        own = slice(r * sources, (r + 1) * sources)
        key = (
            meta[:, 8 * r : 8 * r + 1]
            + DIGIT * meta[:, 8 * r + 1 : 8 * r + 2]
            + DIGIT**2 * meta[:, 8 * r + 2 : 8 * r + 3]
        )
        label = jnp.where(key > label_span, 1.0, jnp.where(key > 0, 0.0, 2.0))
        key_ref[own, :] = jnp.broadcast_to(key, (sources, LANES))
        label_ref[own, :] = jnp.broadcast_to(label, (sources, LANES))
        table = jnp.where(lane == r, key, jnp.where(lane == r + 8, label, table))
    turned_ref[...] = table.T
    here = iota((sources, sources), 0) == iota((sources, sources), 1)
    result = jnp.full((sources, LANES), -1.0, f32)
    tops = jnp.full((8, sources), -1.0, f32)
    halves = sources // LANES
    second = [[jnp.full((8, LANES), minus, f32)] * halves for _ in range(OWN_CAP)]
    first = {}
    tiles = [(r, t) for r in range(OWN_CAP) for t in [r, *range(r)]]
    for m, (r, t) in enumerate(tiles):
        own = slice(r * sources, (r + 1) * sources)
        if t == r:
            for k in range(parts):
                x_ref[own, k * LANES : (k + 1) * LANES] = wide_ref[
                    pl.ds(r * parts + k, sources, stride=stride), :
                ].astype(bf16)
        tile_ref[m] = lax.dot_general(
            x_ref[own, :],
            x_ref[t * sources : (t + 1) * sources, :],
            (((1,), (1,)), ((), ())),
            preferred_element_type=f32,
        )
        if t == r:
            squares = jnp.where(here, tile_ref[m], 0.0)
            scale = lax.rsqrt(jnp.sum(squares, axis=1, keepdims=True) + norm_eps)
            scale_ref[own, :] = jnp.broadcast_to(scale, (sources, LANES))
            turned_ref[16 + r : 17 + r, :] = lax.rsqrt(
                jnp.sum(squares, axis=0, keepdims=True) + norm_eps
            )
        spans = [slice(h * LANES, (h + 1) * LANES) for h in range(halves)]
        label_row = [jnp.broadcast_to(turned_ref[8 + t : 9 + t, c], (8, LANES)) for c in spans]
        key_row = [jnp.broadcast_to(turned_ref[t : t + 1, c], (8, LANES)) for c in spans]
        scale_row = [jnp.broadcast_to(turned_ref[16 + t : 17 + t, c], (8, LANES)) for c in spans]
        for i in range(sources // 8):
            at = slice(r * sources + i * 8, r * sources + i * 8 + 8)
            label_col, key_col = label_ref[at, :], key_ref[at, :]
            if t != r:
                scale_col = scale_ref[at, :]
            forwards = []
            for h in range(halves):
                score = tile_ref[m, i * 8 : (i + 1) * 8, spans[h]]
                score = jnp.where(label_col == label_row[h], score, minus)
                later = key_row[h] < key_col
                forward = jnp.where(later, score * scale_row[h], minus)
                forwards.append(forward)
                if t != r:
                    back = jnp.where(later, minus, score * scale_col)
                    second[t][h] = jnp.maximum(second[t][h], back)
            best = jnp.maximum(*forwards)
            eight = slice(i * 8, i * 8 + 8)
            first_ref[eight, :] = best if t == r else jnp.maximum(first_ref[eight, :], best)
        if m + 1 == len(tiles) or tiles[m + 1][0] != r:
            top = jnp.max(first_ref[...], axis=1, keepdims=True)
            result = jnp.where(lane == r, top * scale_ref[own, :], result)
    for t in range(OWN_CAP):
        top = jnp.concatenate([jnp.max(s, axis=0, keepdims=True) for s in second[t]], axis=1)
        top = top * turned_ref[16 + t : 17 + t, :]
        tops = jnp.where(iota((8, sources), 0) == t, top, tops)
    turned_ref[:8, :] = tops
    result = jnp.maximum(jnp.maximum(result, turned_ref[...].T), -1.0)
    out_ref[...] = result[:, :OWN_CAP]


def pick_kernel(r_ref, named_ref, rank_ref, out_ref):
    owners, rows = named_ref.shape
    padded = jnp.concatenate([r_ref[...], jnp.zeros((owners, LANES - r_ref.shape[1]), f32)], axis=1)
    rest = padded.T[:8, :]
    pieces = []
    for _ in range(3):
        pieces.append(rest.astype(bf16).astype(f32))
        rest = rest - pieces[-1]
    found = jnp.dot(
        jnp.concatenate(pieces, axis=0).astype(bf16), named_ref[...], preferred_element_type=f32
    )
    value = found[:8] + found[8:16] + found[16:]
    value = jnp.where(iota((8, rows), 0) == rank_ref[...], value, 0.0)
    out_ref[...] = jnp.sum(value, axis=0, keepdims=True)


def call(kernel, out_shape, scratch, name, **rest):
    return pl.pallas_call(
        kernel,
        out_shape=out_shape,
        scratch_shapes=scratch,
        compiler_params=pltpu.CompilerParams(vmem_limit_bytes=48 * 2**20),
        name=name,
        **rest,
    )


def stay(value):
    return pltpu.with_memory_space_constraint(value, pltpu.HBM)


def shards(embeddings, clusters, priorities):
    rows, width = embeddings.shape
    owners = lax.axis_size(ORDER)
    label_span = rows * owners
    height = owners * (OWN_CAP * width // LANES + META)
    slots = owners * OWN_CAP
    wide = pltpu.VMEM((height, LANES), f32)
    packed, named, rank = call(
        functools.partial(pack_kernel, label_span),
        (
            jax.ShapeDtypeStruct((height, LANES), bf16),
            jax.ShapeDtypeStruct((owners, rows), bf16),
            jax.ShapeDtypeStruct((1, rows), jnp.int32),
        ),
        [
            wide,
            pltpu.VMEM((1, rows), jnp.int32),
            pltpu.VMEM((1, rows), jnp.int32),
            pltpu.VMEM((rows, width), bf16),
            pltpu.SemaphoreType.DMA((2 + X_PIECES,)),
            pltpu.VMEM((slots, rows), bf16),
            pltpu.VMEM((owners, rows), f32),
        ],
        "pack",
        in_specs=[pl.BlockSpec(memory_space=pltpu.HBM)] * 3,
    )(stay(clusters.reshape(1, rows)), stay(priorities.reshape(1, rows)), stay(embeddings))
    arrived = lax.all_to_all(
        packed.reshape(owners, height // owners // 2, 2, LANES),
        ORDER,
        split_axis=0,
        concat_axis=0,
        tiled=True,
    ).reshape(height, LANES)
    result = call(
        functools.partial(score_kernel, label_span),
        jax.ShapeDtypeStruct((owners, OWN_CAP), f32),
        [
            wide,
            pltpu.VMEM((slots, width), bf16),
            pltpu.VMEM((slots, LANES), f32),
            pltpu.VMEM((slots, LANES), f32),
            pltpu.VMEM((slots, LANES), f32),
            pltpu.VMEM((LANES, owners), f32),
            pltpu.VMEM((OWN_CAP * (OWN_CAP + 1) // 2, owners, owners), f32),
            pltpu.VMEM((owners, LANES), f32),
        ],
        "score",
    )(arrived)
    returned = lax.all_to_all(result, ORDER, split_axis=0, concat_axis=0, tiled=True)
    best = call(pick_kernel, jax.ShapeDtypeStruct((1, rows), f32), [], "pick")(returned, named, rank)
    return best.reshape(rows)


def solution(mesh):
    fine = Mesh(mesh.devices.reshape(-1, *PLACE, mesh.shape["gy"]), AXES)
    in_specs = (P(AXES, None), P(AXES), P(AXES))
    return jax.shard_map(shards, mesh=fine, in_specs=in_specs, out_specs=P(AXES), check_vma=False)
```

```python
import functools

import jax
import jax.numpy as jnp
from jax import lax
from jax.experimental import pallas as pl
from jax.experimental.pallas import tpu as pltpu
from jax.sharding import Mesh
from jax.sharding import PartitionSpec as P

CLUS_DEV = 2
OWN_CAP = 6
LANES = 128
AXES = ("z", "x", "core", "gy")
PLACE = (4, 2)
ORDER = ("core", "x", "gy", "z")
BACK = ("z", "core", "x", "gy")
META = 2
DIGIT = 128
X_PIECES = 1
GROUPS = 2

norm_eps = 1e-06
bf16 = jnp.bfloat16
f32 = jnp.float32


def iota(shape, dim):
    return lax.broadcasted_iota(jnp.int32, shape, dim)


def pack_kernel(
    label_span,
    depth,
    c_hbm,
    p_hbm,
    x_hbm,
    w_ref,
    named_ref,
    rank_ref,
    wide_ref,
    c_ref,
    p_ref,
    x_ref,
    sems,
    pick_ref,
    slot_ref,
):
    owners, rows = slot_ref.shape
    width = x_ref.shape[1]
    parts = width // LANES
    stride = w_ref.shape[0] // owners
    block = min(512, rows)
    copies = [
        pltpu.make_async_copy(c_hbm, c_ref, sems.at[0]),
        pltpu.make_async_copy(p_hbm, p_ref, sems.at[1]),
    ]
    piece = rows // X_PIECES
    for i in range(X_PIECES):
        span = pl.ds(i * piece, piece)
        copies.append(pltpu.make_async_copy(x_hbm.at[span], x_ref.at[span], sems.at[2 + i]))
    for copy in copies:
        copy.start()
    before = (iota((block, block), 0) < iota((block, block), 1)).astype(f32).astype(bf16)
    copies[0].wait()
    copies[1].wait()
    clusters = c_ref[...]
    owner = clusters // CLUS_DEV
    key = (clusters % CLUS_DEV) * label_span + p_ref[...] + 1
    carry = jnp.zeros((owners, 1), f32)
    for b in range(rows // block):
        cols = slice(b * block, (b + 1) * block)
        named = iota((owners, block), 0) == owner[:, cols]
        count = named.astype(f32)
        rank = jnp.dot(count.astype(bf16), before, preferred_element_type=f32) + carry
        carry = carry + jnp.sum(count, axis=1, keepdims=True)
        slot_ref[:, cols] = jnp.where(named, rank, -1.0)
        turn = iota((owners, block), 0)
        turn = turn % (owners // depth) * depth + turn // (owners // depth)
        named_ref[:, cols] = (turn == owner[:, cols]).astype(f32).astype(bf16)
        place = jnp.sum(jnp.where(named, rank, 0.0), axis=0, keepdims=True)
        rank_ref[:, cols] = place.astype(jnp.int32)
    key = key.astype(f32)
    lane = iota((owners, LANES), 1)
    for copy in copies[2:]:
        copy.wait()
    group = owners // GROUPS
    for g in range(GROUPS):
        some = slice(g * group, (g + 1) * group)
        for q in range(OWN_CAP):
            hit = slot_ref[some, :] == q
            at = (g * OWN_CAP + q) * group
            pick_ref[at : at + group, :] = jnp.where(hit, 1.0, 0.0).astype(bf16)
            held = jnp.sum(jnp.where(hit, key, 0.0), axis=1, keepdims=True)
            table_g = jnp.where(lane[some] // 8 == q, held, 0.0 if q == 0 else table_g)
        picked = jnp.dot(
            pick_ref[g * OWN_CAP * group : (g + 1) * OWN_CAP * group, :],
            x_ref[...],
            preferred_element_type=f32,
        )
        for q in range(OWN_CAP):
            for k in range(parts):
                wide_ref[pl.ds(g * group * stride + q * parts + k, group, stride=stride), :] = picked[
                    q * group : (q + 1) * group, k * LANES : (k + 1) * LANES
                ]
        table_g = table_g.astype(jnp.int32)
        kind = lane[some] % 8
        meta = jnp.where(
            kind == 0,
            table_g % DIGIT,
            jnp.where(
                kind == 1,
                table_g // DIGIT % DIGIT,
                jnp.where(kind == 2, table_g // DIGIT**2, 0),
            ),
        ).astype(f32)
        at = g * group * stride + OWN_CAP * parts
        wide_ref[pl.ds(at, group, stride=stride), :] = meta
        wide_ref[pl.ds(at + 1, group, stride=stride), :] = jnp.zeros_like(meta)
        whole = slice(g * group * stride, (g + 1) * group * stride)
        w_ref[whole, :] = wide_ref[whole, :].astype(bf16)


def score_kernel(
    label_span,
    depth,
    w_ref,
    out_ref,
    wide_ref,
    x_ref,
    key_ref,
    label_ref,
    scale_ref,
    turned_ref,
    tile_ref,
    first_ref,
):
    sources = out_ref.shape[0]
    width = x_ref.shape[1]
    parts = width // LANES
    stride = w_ref.shape[0] // sources
    minus = -jnp.inf
    wide_ref[...] = w_ref[...].astype(f32)
    meta = wide_ref[pl.ds(OWN_CAP * parts, sources, stride=stride), :]
    lane = iota((sources, LANES), 1)
    table = jnp.zeros((sources, LANES), f32)
    for r in range(OWN_CAP):
        own = slice(r * sources, (r + 1) * sources)
        key = (
            meta[:, 8 * r : 8 * r + 1]
            + DIGIT * meta[:, 8 * r + 1 : 8 * r + 2]
            + DIGIT**2 * meta[:, 8 * r + 2 : 8 * r + 3]
        )
        label = jnp.where(key > label_span, 1.0, jnp.where(key > 0, 0.0, 2.0))
        key_ref[own, :] = jnp.broadcast_to(key, (sources, LANES))
        label_ref[own, :] = jnp.broadcast_to(label, (sources, LANES))
        table = jnp.where(lane == r, key, jnp.where(lane == r + 8, label, table))
    turned_ref[...] = table.T
    here = iota((sources, sources), 0) == iota((sources, sources), 1)
    result = jnp.full((sources, LANES), -1.0, f32)
    tops = jnp.full((8, sources), -1.0, f32)
    halves = sources // LANES
    second = [[jnp.full((8, LANES), minus, f32)] * halves for _ in range(OWN_CAP)]
    first = {}
    tiles = [(r, t) for r in range(OWN_CAP) for t in [r, *range(r)]]
    for m, (r, t) in enumerate(tiles):
        own = slice(r * sources, (r + 1) * sources)
        if t == r:
            for k in range(parts):
                x_ref[own, k * LANES : (k + 1) * LANES] = wide_ref[
                    pl.ds(r * parts + k, sources, stride=stride), :
                ].astype(bf16)
        tile_ref[m] = lax.dot_general(
            x_ref[own, :],
            x_ref[t * sources : (t + 1) * sources, :],
            (((1,), (1,)), ((), ())),
            preferred_element_type=f32,
        )
        if t == r:
            squares = jnp.where(here, tile_ref[m], 0.0)
            scale = lax.rsqrt(jnp.sum(squares, axis=1, keepdims=True) + norm_eps)
            scale_ref[own, :] = jnp.broadcast_to(scale, (sources, LANES))
            turned_ref[16 + r : 17 + r, :] = lax.rsqrt(
                jnp.sum(squares, axis=0, keepdims=True) + norm_eps
            )
        spans = [slice(h * LANES, (h + 1) * LANES) for h in range(halves)]
        label_row = [jnp.broadcast_to(turned_ref[8 + t : 9 + t, c], (8, LANES)) for c in spans]
        key_row = [jnp.broadcast_to(turned_ref[t : t + 1, c], (8, LANES)) for c in spans]
        scale_row = [jnp.broadcast_to(turned_ref[16 + t : 17 + t, c], (8, LANES)) for c in spans]
        for i in range(sources // 8):
            at = slice(r * sources + i * 8, r * sources + i * 8 + 8)
            label_col, key_col = label_ref[at, :], key_ref[at, :]
            if t != r:
                scale_col = scale_ref[at, :]
            forwards = []
            for h in range(halves):
                score = tile_ref[m, i * 8 : (i + 1) * 8, spans[h]]
                score = jnp.where(label_col == label_row[h], score, minus)
                later = key_row[h] < key_col
                forward = jnp.where(later, score * scale_row[h], minus)
                forwards.append(forward)
                if t != r:
                    back = jnp.where(later, minus, score * scale_col)
                    second[t][h] = jnp.maximum(second[t][h], back)
            best = jnp.maximum(*forwards)
            eight = slice(i * 8, i * 8 + 8)
            first_ref[eight, :] = best if t == r else jnp.maximum(first_ref[eight, :], best)
        if m + 1 == len(tiles) or tiles[m + 1][0] != r:
            top = jnp.max(first_ref[...], axis=1, keepdims=True)
            result = jnp.where(lane == r, top * scale_ref[own, :], result)
    for t in range(OWN_CAP):
        top = jnp.concatenate([jnp.max(s, axis=0, keepdims=True) for s in second[t]], axis=1)
        top = top * turned_ref[16 + t : 17 + t, :]
        tops = jnp.where(iota((8, sources), 0) == t, top, tops)
    turned_ref[:8, :] = tops
    result = jnp.maximum(jnp.maximum(result, turned_ref[...].T), -1.0)
    first_ref[...] = result
    plane = sources // depth
    for z in range(depth):
        part = first_ref[pl.ds(z, plane, stride=depth), :]
        out_ref[z * plane : (z + 1) * plane, :] = part[:, :OWN_CAP]


def pick_kernel(r_ref, named_ref, rank_ref, out_ref):
    owners, rows = named_ref.shape
    padded = jnp.concatenate([r_ref[...], jnp.zeros((owners, LANES - r_ref.shape[1]), f32)], axis=1)
    rest = padded.T[:8, :]
    pieces = []
    for _ in range(3):
        pieces.append(rest.astype(bf16).astype(f32))
        rest = rest - pieces[-1]
    found = jnp.dot(
        jnp.concatenate(pieces, axis=0).astype(bf16), named_ref[...], preferred_element_type=f32
    )
    value = found[:8] + found[8:16] + found[16:]
    value = jnp.where(iota((8, rows), 0) == rank_ref[...], value, 0.0)
    out_ref[...] = jnp.sum(value, axis=0, keepdims=True)


def call(kernel, out_shape, scratch, name, **rest):
    return pl.pallas_call(
        kernel,
        out_shape=out_shape,
        scratch_shapes=scratch,
        compiler_params=pltpu.CompilerParams(vmem_limit_bytes=48 * 2**20),
        name=name,
        **rest,
    )


def stay(value):
    return pltpu.with_memory_space_constraint(value, pltpu.HBM)


def shards(embeddings, clusters, priorities):
    rows, width = embeddings.shape
    owners = lax.axis_size(ORDER)
    depth = lax.axis_size("z")
    label_span = rows * owners
    height = owners * (OWN_CAP * width // LANES + META)
    slots = owners * OWN_CAP
    wide = pltpu.VMEM((height, LANES), f32)
    packed, named, rank = call(
        functools.partial(pack_kernel, label_span, depth),
        (
            jax.ShapeDtypeStruct((height, LANES), bf16),
            jax.ShapeDtypeStruct((owners, rows), bf16),
            jax.ShapeDtypeStruct((1, rows), jnp.int32),
        ),
        [
            wide,
            pltpu.VMEM((1, rows), jnp.int32),
            pltpu.VMEM((1, rows), jnp.int32),
            pltpu.VMEM((rows, width), bf16),
            pltpu.SemaphoreType.DMA((2 + X_PIECES,)),
            pltpu.VMEM((slots, rows), bf16),
            pltpu.VMEM((owners, rows), f32),
        ],
        "pack",
        in_specs=[pl.BlockSpec(memory_space=pltpu.HBM)] * 3,
    )(stay(clusters.reshape(1, rows)), stay(priorities.reshape(1, rows)), stay(embeddings))
    arrived = lax.all_to_all(
        packed.reshape(owners, height // owners // 2, 2, LANES),
        ORDER,
        split_axis=0,
        concat_axis=0,
        tiled=True,
    ).reshape(height, LANES)
    result = call(
        functools.partial(score_kernel, label_span, depth),
        jax.ShapeDtypeStruct((owners, OWN_CAP), f32),
        [
            wide,
            pltpu.VMEM((slots, width), bf16),
            pltpu.VMEM((slots, LANES), f32),
            pltpu.VMEM((slots, LANES), f32),
            pltpu.VMEM((slots, LANES), f32),
            pltpu.VMEM((LANES, owners), f32),
            pltpu.VMEM((OWN_CAP * (OWN_CAP + 1) // 2, owners, owners), f32),
            pltpu.VMEM((owners, LANES), f32),
        ],
        "score",
    )(arrived)
    returned = lax.all_to_all(result, BACK, split_axis=0, concat_axis=0, tiled=True)
    best = call(pick_kernel, jax.ShapeDtypeStruct((1, rows), f32), [], "pick")(returned, named, rank)
    return best.reshape(rows)


def solution(mesh):
    fine = Mesh(mesh.devices.reshape(-1, *PLACE, mesh.shape["gy"]), AXES)
    in_specs = (P(AXES, None), P(AXES), P(AXES))
    return jax.shard_map(shards, mesh=fine, in_specs=in_specs, out_specs=P(AXES), check_vma=False)
```

```python
import functools

import jax
import jax.numpy as jnp
from jax import lax
from jax.experimental import pallas as pl
from jax.experimental.pallas import tpu as pltpu
from jax.sharding import PartitionSpec as P

CLUS_DEV = 2
OWN_CAP = 6
LANES = 128
META = 2
DIGIT = 128
X_PIECES = 1
GROUPS = 2

norm_eps = 1e-06
bf16 = jnp.bfloat16
f32 = jnp.float32


def iota(shape, dim):
    return lax.broadcasted_iota(jnp.int32, shape, dim)


def pack_kernel(
    label_span,
    c_hbm,
    p_hbm,
    x_hbm,
    w_ref,
    named_ref,
    rank_ref,
    wide_ref,
    c_ref,
    p_ref,
    x_ref,
    sems,
    pick_ref,
    slot_ref,
):
    owners, rows = slot_ref.shape
    width = x_ref.shape[1]
    parts = width // LANES
    stride = w_ref.shape[0] // owners
    block = min(512, rows)
    copies = [
        pltpu.make_async_copy(c_hbm, c_ref, sems.at[0]),
        pltpu.make_async_copy(p_hbm, p_ref, sems.at[1]),
    ]
    piece = rows // X_PIECES
    for i in range(X_PIECES):
        span = pl.ds(i * piece, piece)
        copies.append(pltpu.make_async_copy(x_hbm.at[span], x_ref.at[span], sems.at[2 + i]))
    for copy in copies:
        copy.start()
    before = (iota((block, block), 0) < iota((block, block), 1)).astype(f32).astype(bf16)
    copies[0].wait()
    copies[1].wait()
    clusters = c_ref[...]
    owner = clusters // CLUS_DEV
    key = (clusters % CLUS_DEV) * label_span + p_ref[...] + 1
    carry = jnp.zeros((owners, 1), f32)
    for b in range(rows // block):
        cols = slice(b * block, (b + 1) * block)
        named = iota((owners, block), 0) == owner[:, cols]
        count = named.astype(f32)
        rank = jnp.dot(count.astype(bf16), before, preferred_element_type=f32) + carry
        carry = carry + jnp.sum(count, axis=1, keepdims=True)
        slot_ref[:, cols] = jnp.where(named, rank, -1.0)
        named_ref[:, cols] = count.astype(bf16)
        place = jnp.sum(jnp.where(named, rank, 0.0), axis=0, keepdims=True)
        rank_ref[:, cols] = place.astype(jnp.int32)
    key = key.astype(f32)
    lane = iota((owners, LANES), 1)
    for copy in copies[2:]:
        copy.wait()
    group = owners // GROUPS
    for g in range(GROUPS):
        some = slice(g * group, (g + 1) * group)
        for q in range(OWN_CAP):
            hit = slot_ref[some, :] == q
            at = (g * OWN_CAP + q) * group
            pick_ref[at : at + group, :] = jnp.where(hit, 1.0, 0.0).astype(bf16)
            held = jnp.sum(jnp.where(hit, key, 0.0), axis=1, keepdims=True)
            table_g = jnp.where(lane[some] // 8 == q, held, 0.0 if q == 0 else table_g)
        picked = jnp.dot(
            pick_ref[g * OWN_CAP * group : (g + 1) * OWN_CAP * group, :],
            x_ref[...],
            preferred_element_type=f32,
        )
        for q in range(OWN_CAP):
            for k in range(parts):
                wide_ref[pl.ds(g * group * stride + q * parts + k, group, stride=stride), :] = picked[
                    q * group : (q + 1) * group, k * LANES : (k + 1) * LANES
                ]
        table_g = table_g.astype(jnp.int32)
        kind = lane[some] % 8
        meta = jnp.where(
            kind == 0,
            table_g % DIGIT,
            jnp.where(
                kind == 1,
                table_g // DIGIT % DIGIT,
                jnp.where(kind == 2, table_g // DIGIT**2, 0),
            ),
        ).astype(f32)
        at = g * group * stride + OWN_CAP * parts
        wide_ref[pl.ds(at, group, stride=stride), :] = meta
        wide_ref[pl.ds(at + 1, group, stride=stride), :] = jnp.zeros_like(meta)
        whole = slice(g * group * stride, (g + 1) * group * stride)
        w_ref[whole, :] = wide_ref[whole, :].astype(bf16)


def score_kernel(
    label_span,
    w_ref,
    out_ref,
    wide_ref,
    x_ref,
    key_ref,
    label_ref,
    scale_ref,
    turned_ref,
    tile_ref,
    first_ref,
):
    sources = out_ref.shape[0]
    width = x_ref.shape[1]
    parts = width // LANES
    stride = w_ref.shape[0] // sources
    minus = -jnp.inf
    wide_ref[...] = w_ref[...].astype(f32)
    meta = wide_ref[pl.ds(OWN_CAP * parts, sources, stride=stride), :]
    lane = iota((sources, LANES), 1)
    table = jnp.zeros((sources, LANES), f32)
    for r in range(OWN_CAP):
        own = slice(r * sources, (r + 1) * sources)
        key = (
            meta[:, 8 * r : 8 * r + 1]
            + DIGIT * meta[:, 8 * r + 1 : 8 * r + 2]
            + DIGIT**2 * meta[:, 8 * r + 2 : 8 * r + 3]
        )
        label = jnp.where(key > label_span, 1.0, jnp.where(key > 0, 0.0, 2.0))
        key_ref[own, :] = jnp.broadcast_to(key, (sources, LANES))
        label_ref[own, :] = jnp.broadcast_to(label, (sources, LANES))
        table = jnp.where(lane == r, key, jnp.where(lane == r + 8, label, table))
    turned_ref[...] = table.T
    here = iota((sources, sources), 0) == iota((sources, sources), 1)
    result = jnp.full((sources, LANES), -1.0, f32)
    tops = jnp.full((8, sources), -1.0, f32)
    halves = sources // LANES
    second = [[jnp.full((8, LANES), minus, f32)] * halves for _ in range(OWN_CAP)]
    first = {}
    spans = [slice(h * LANES, (h + 1) * LANES) for h in range(halves)]
    for r in range(OWN_CAP):
        own = slice(r * sources, (r + 1) * sources)
        for k in range(parts):
            x_ref[own, k * LANES : (k + 1) * LANES] = wide_ref[
                pl.ds(r * parts + k, sources, stride=stride), :
            ].astype(bf16)
        order = [r, *range(r)]
        for t in order:
            tile_ref[t] = lax.dot_general(
                x_ref[own, :],
                x_ref[t * sources : (t + 1) * sources, :],
                (((1,), (1,)), ((), ())),
                preferred_element_type=f32,
            )
            if t == r:
                squares = jnp.where(here, tile_ref[t], 0.0)
                scale = lax.rsqrt(jnp.sum(squares, axis=1, keepdims=True) + norm_eps)
                scale_ref[own, :] = jnp.broadcast_to(scale, (sources, LANES))
                turned_ref[16 + r : 17 + r, :] = lax.rsqrt(
                    jnp.sum(squares, axis=0, keepdims=True) + norm_eps
                )
        for i in range(0, sources, 32):
            subs = [slice(r * sources + i + j, r * sources + i + j + 8) for j in range(0, 32, 8)]
            label_col = [label_ref[at, :] for at in subs]
            key_col = [key_ref[at, :] for at in subs]
            scale_col = [scale_ref[at, :] for at in subs]
            best = [None] * len(subs)
            for t in order:
                for h, c in enumerate(spans):
                    key_row = jnp.broadcast_to(turned_ref[t : t + 1, c], (8, LANES))
                    label_row = jnp.broadcast_to(turned_ref[8 + t : 9 + t, c], (8, LANES))
                    scale_row = jnp.broadcast_to(turned_ref[16 + t : 17 + t, c], (8, LANES))
                    for j in range(len(subs)):
                        score = tile_ref[t, i + 8 * j : i + 8 * j + 8, c]
                        score = jnp.where(label_col[j] == label_row, score, minus)
                        later = key_row < key_col[j]
                        forward = jnp.where(later, score * scale_row, minus)
                        best[j] = forward if best[j] is None else jnp.maximum(best[j], forward)
                        if t != r:
                            back = jnp.where(later, minus, score * scale_col[j])
                            second[t][h] = jnp.maximum(second[t][h], back)
            for j in range(len(subs)):
                first_ref[i + 8 * j : i + 8 * j + 8, :] = best[j]
        top = jnp.max(first_ref[...], axis=1, keepdims=True)
        result = jnp.where(lane == r, top * scale_ref[own, :], result)
    for t in range(OWN_CAP):
        top = jnp.concatenate([jnp.max(s, axis=0, keepdims=True) for s in second[t]], axis=1)
        top = top * turned_ref[16 + t : 17 + t, :]
        tops = jnp.where(iota((8, sources), 0) == t, top, tops)
    turned_ref[:8, :] = tops
    result = jnp.maximum(jnp.maximum(result, turned_ref[...].T), -1.0)
    out_ref[...] = result[:, :OWN_CAP]


def pick_kernel(r_ref, named_ref, rank_ref, out_ref):
    owners, rows = named_ref.shape
    padded = jnp.concatenate([r_ref[...], jnp.zeros((owners, LANES - r_ref.shape[1]), f32)], axis=1)
    rest = padded.T[:8, :]
    pieces = []
    for _ in range(3):
        pieces.append(rest.astype(bf16).astype(f32))
        rest = rest - pieces[-1]
    found = jnp.dot(
        jnp.concatenate(pieces, axis=0).astype(bf16), named_ref[...], preferred_element_type=f32
    )
    value = found[:8] + found[8:16] + found[16:]
    value = jnp.where(iota((8, rows), 0) == rank_ref[...], value, 0.0)
    out_ref[...] = jnp.sum(value, axis=0, keepdims=True)


def call(kernel, out_shape, scratch, name, **rest):
    return pl.pallas_call(
        kernel,
        out_shape=out_shape,
        scratch_shapes=scratch,
        compiler_params=pltpu.CompilerParams(vmem_limit_bytes=48 * 2**20),
        name=name,
        **rest,
    )


def stay(value):
    return pltpu.with_memory_space_constraint(value, pltpu.HBM)


def shards(embeddings, clusters, priorities):
    rows, width = embeddings.shape
    owners = lax.axis_size("gx") * lax.axis_size("gy")
    label_span = rows * owners
    height = owners * (OWN_CAP * width // LANES + META)
    slots = owners * OWN_CAP
    wide = pltpu.VMEM((height, LANES), f32)
    packed, named, rank = call(
        functools.partial(pack_kernel, label_span),
        (
            jax.ShapeDtypeStruct((height, LANES), bf16),
            jax.ShapeDtypeStruct((owners, rows), bf16),
            jax.ShapeDtypeStruct((1, rows), jnp.int32),
        ),
        [
            wide,
            pltpu.VMEM((1, rows), jnp.int32),
            pltpu.VMEM((1, rows), jnp.int32),
            pltpu.VMEM((rows, width), bf16),
            pltpu.SemaphoreType.DMA((2 + X_PIECES,)),
            pltpu.VMEM((slots, rows), bf16),
            pltpu.VMEM((owners, rows), f32),
        ],
        "pack",
        in_specs=[pl.BlockSpec(memory_space=pltpu.HBM)] * 3,
    )(stay(clusters.reshape(1, rows)), stay(priorities.reshape(1, rows)), stay(embeddings))
    arrived = lax.all_to_all(
        packed.reshape(owners, height // owners // 2, 2, LANES),
        ("gx", "gy"),
        split_axis=0,
        concat_axis=0,
        tiled=True,
    ).reshape(height, LANES)
    result = call(
        functools.partial(score_kernel, label_span),
        jax.ShapeDtypeStruct((owners, OWN_CAP), f32),
        [
            wide,
            pltpu.VMEM((slots, width), bf16),
            pltpu.VMEM((slots, LANES), f32),
            pltpu.VMEM((slots, LANES), f32),
            pltpu.VMEM((slots, LANES), f32),
            pltpu.VMEM((LANES, owners), f32),
            pltpu.VMEM((OWN_CAP * (OWN_CAP + 1) // 2, owners, owners), f32),
            pltpu.VMEM((owners, LANES), f32),
        ],
        "score",
    )(arrived)
    returned = lax.all_to_all(result, ("gx", "gy"), split_axis=0, concat_axis=0, tiled=True)
    best = call(pick_kernel, jax.ShapeDtypeStruct((1, rows), f32), [], "pick")(returned, named, rank)
    return best.reshape(rows)


def solution(mesh):
    in_specs = (P(("gx", "gy"), None), P(("gx", "gy")), P(("gx", "gy")))
    out_specs = P(("gx", "gy"))
    return jax.shard_map(shards, mesh=mesh, in_specs=in_specs, out_specs=out_specs, check_vma=False)
```

```python
import functools

import jax
import jax.numpy as jnp
from jax import lax
from jax.experimental import pallas as pl
from jax.experimental.pallas import tpu as pltpu
from jax.sharding import Mesh
from jax.sharding import PartitionSpec as P

CLUS_DEV = 2
OWN_CAP = 6
LANES = 128
AXES = ("z", "x", "core", "gy")
PLACE = (4, 2)
ORDER = ("core", "gy", "z", "x")
META = 2
DIGIT = 128
X_PIECES = 1
GROUPS = 2

norm_eps = 1e-06
bf16 = jnp.bfloat16
f32 = jnp.float32


def iota(shape, dim):
    return lax.broadcasted_iota(jnp.int32, shape, dim)


def pack_kernel(
    label_span,
    c_hbm,
    p_hbm,
    x_hbm,
    w_ref,
    named_ref,
    rank_ref,
    wide_ref,
    c_ref,
    p_ref,
    x_ref,
    sems,
    pick_ref,
    slot_ref,
):
    owners, rows = slot_ref.shape
    width = x_ref.shape[1]
    parts = width // LANES
    stride = w_ref.shape[0] // owners
    block = min(512, rows)
    copies = [
        pltpu.make_async_copy(c_hbm, c_ref, sems.at[0]),
        pltpu.make_async_copy(p_hbm, p_ref, sems.at[1]),
    ]
    piece = rows // X_PIECES
    for i in range(X_PIECES):
        span = pl.ds(i * piece, piece)
        copies.append(pltpu.make_async_copy(x_hbm.at[span], x_ref.at[span], sems.at[2 + i]))
    for copy in copies:
        copy.start()
    before = (iota((block, block), 0) < iota((block, block), 1)).astype(f32).astype(bf16)
    copies[0].wait()
    copies[1].wait()
    clusters = c_ref[...]
    owner = clusters // CLUS_DEV
    key = (clusters % CLUS_DEV) * label_span + p_ref[...] + 1
    carry = jnp.zeros((owners, 1), f32)
    for b in range(rows // block):
        cols = slice(b * block, (b + 1) * block)
        named = iota((owners, block), 0) == owner[:, cols]
        count = named.astype(f32)
        rank = jnp.dot(count.astype(bf16), before, preferred_element_type=f32) + carry
        carry = carry + jnp.sum(count, axis=1, keepdims=True)
        slot_ref[:, cols] = jnp.where(named, rank, -1.0)
        named_ref[:, cols] = count.astype(bf16)
        place = jnp.sum(jnp.where(named, rank, 0.0), axis=0, keepdims=True)
        rank_ref[:, cols] = place.astype(jnp.int32)
    key = key.astype(f32)
    lane = iota((owners, LANES), 1)
    for copy in copies[2:]:
        copy.wait()
    group = owners // GROUPS
    for g in range(GROUPS):
        some = slice(g * group, (g + 1) * group)
        for q in range(OWN_CAP):
            hit = slot_ref[some, :] == q
            at = (g * OWN_CAP + q) * group
            pick_ref[at : at + group, :] = jnp.where(hit, 1.0, 0.0).astype(bf16)
            held = jnp.sum(jnp.where(hit, key, 0.0), axis=1, keepdims=True)
            table_g = jnp.where(lane[some] // 8 == q, held, 0.0 if q == 0 else table_g)
        picked = jnp.dot(
            pick_ref[g * OWN_CAP * group : (g + 1) * OWN_CAP * group, :],
            x_ref[...],
            preferred_element_type=f32,
        )
        for q in range(OWN_CAP):
            for k in range(parts):
                wide_ref[pl.ds(g * group * stride + q * parts + k, group, stride=stride), :] = picked[
                    q * group : (q + 1) * group, k * LANES : (k + 1) * LANES
                ]
        table_g = table_g.astype(jnp.int32)
        kind = lane[some] % 8
        meta = jnp.where(
            kind == 0,
            table_g % DIGIT,
            jnp.where(
                kind == 1,
                table_g // DIGIT % DIGIT,
                jnp.where(kind == 2, table_g // DIGIT**2, 0),
            ),
        ).astype(f32)
        at = g * group * stride + OWN_CAP * parts
        wide_ref[pl.ds(at, group, stride=stride), :] = meta
        wide_ref[pl.ds(at + 1, group, stride=stride), :] = jnp.zeros_like(meta)
        whole = slice(g * group * stride, (g + 1) * group * stride)
        w_ref[whole, :] = wide_ref[whole, :].astype(bf16)


def score_kernel(
    label_span,
    w_ref,
    out_ref,
    wide_ref,
    x_ref,
    key_ref,
    label_ref,
    scale_ref,
    turned_ref,
    tile_ref,
    first_ref,
):
    sources = out_ref.shape[0]
    width = x_ref.shape[1]
    parts = width // LANES
    stride = w_ref.shape[0] // sources
    minus = -jnp.inf
    wide_ref[...] = w_ref[...].astype(f32)
    meta = wide_ref[pl.ds(OWN_CAP * parts, sources, stride=stride), :]
    lane = iota((sources, LANES), 1)
    table = jnp.zeros((sources, LANES), f32)
    for r in range(OWN_CAP):
        own = slice(r * sources, (r + 1) * sources)
        key = (
            meta[:, 8 * r : 8 * r + 1]
            + DIGIT * meta[:, 8 * r + 1 : 8 * r + 2]
            + DIGIT**2 * meta[:, 8 * r + 2 : 8 * r + 3]
        )
        label = jnp.where(key > label_span, 1.0, jnp.where(key > 0, 0.0, 2.0))
        key_ref[own, :] = jnp.broadcast_to(key, (sources, LANES))
        label_ref[own, :] = jnp.broadcast_to(label, (sources, LANES))
        table = jnp.where(lane == r, key, jnp.where(lane == r + 8, label, table))
    turned_ref[...] = table.T
    here = iota((sources, sources), 0) == iota((sources, sources), 1)
    result = jnp.full((sources, LANES), -1.0, f32)
    tops = jnp.full((8, sources), -1.0, f32)
    halves = sources // LANES
    second = [[jnp.full((8, LANES), minus, f32)] * halves for _ in range(OWN_CAP)]
    first = {}
    tiles = [(r, t) for r in range(OWN_CAP) for t in [r, *range(r)]]
    for m, (r, t) in enumerate(tiles):
        own = slice(r * sources, (r + 1) * sources)
        if t == r:
            for k in range(parts):
                x_ref[own, k * LANES : (k + 1) * LANES] = wide_ref[
                    pl.ds(r * parts + k, sources, stride=stride), :
                ].astype(bf16)
        tile_ref[m] = lax.dot_general(
            x_ref[own, :],
            x_ref[t * sources : (t + 1) * sources, :],
            (((1,), (1,)), ((), ())),
            preferred_element_type=f32,
        )
        if t == r:
            squares = jnp.where(here, tile_ref[m], 0.0)
            scale = lax.rsqrt(jnp.sum(squares, axis=1, keepdims=True) + norm_eps)
            scale_ref[own, :] = jnp.broadcast_to(scale, (sources, LANES))
            turned_ref[16 + r : 17 + r, :] = lax.rsqrt(
                jnp.sum(squares, axis=0, keepdims=True) + norm_eps
            )
        spans = [slice(h * LANES, (h + 1) * LANES) for h in range(halves)]
        label_row = [jnp.broadcast_to(turned_ref[8 + t : 9 + t, c], (8, LANES)) for c in spans]
        key_row = [jnp.broadcast_to(turned_ref[t : t + 1, c], (8, LANES)) for c in spans]
        scale_row = [jnp.broadcast_to(turned_ref[16 + t : 17 + t, c], (8, LANES)) for c in spans]
        for i in range(sources // 8):
            at = slice(r * sources + i * 8, r * sources + i * 8 + 8)
            label_col, key_col = label_ref[at, :], key_ref[at, :]
            if t != r:
                scale_col = scale_ref[at, :]
            forwards = []
            for h in range(halves):
                score = tile_ref[m, i * 8 : (i + 1) * 8, spans[h]]
                score = jnp.where(label_col == label_row[h], score, minus)
                later = key_row[h] < key_col
                forward = jnp.where(later, score * scale_row[h], minus)
                forwards.append(forward)
                if t != r:
                    back = jnp.where(later, minus, score * scale_col)
                    second[t][h] = jnp.maximum(second[t][h], back)
            best = jnp.maximum(*forwards)
            eight = slice(i * 8, i * 8 + 8)
            first_ref[eight, :] = best if t == r else jnp.maximum(first_ref[eight, :], best)
        if m + 1 == len(tiles) or tiles[m + 1][0] != r:
            top = jnp.max(first_ref[...], axis=1, keepdims=True)
            result = jnp.where(lane == r, top * scale_ref[own, :], result)
    for t in range(OWN_CAP):
        top = jnp.concatenate([jnp.max(s, axis=0, keepdims=True) for s in second[t]], axis=1)
        top = top * turned_ref[16 + t : 17 + t, :]
        tops = jnp.where(iota((8, sources), 0) == t, top, tops)
    turned_ref[:8, :] = tops
    result = jnp.maximum(jnp.maximum(result, turned_ref[...].T), -1.0)
    out_ref[...] = result[:, :OWN_CAP]


def pick_kernel(r_ref, named_ref, rank_ref, out_ref):
    owners, rows = named_ref.shape
    padded = jnp.concatenate([r_ref[...], jnp.zeros((owners, LANES - r_ref.shape[1]), f32)], axis=1)
    rest = padded.T[:8, :]
    pieces = []
    for _ in range(3):
        pieces.append(rest.astype(bf16).astype(f32))
        rest = rest - pieces[-1]
    found = jnp.dot(
        jnp.concatenate(pieces, axis=0).astype(bf16), named_ref[...], preferred_element_type=f32
    )
    value = found[:8] + found[8:16] + found[16:]
    value = jnp.where(iota((8, rows), 0) == rank_ref[...], value, 0.0)
    out_ref[...] = jnp.sum(value, axis=0, keepdims=True)


def call(kernel, out_shape, scratch, name, **rest):
    return pl.pallas_call(
        kernel,
        out_shape=out_shape,
        scratch_shapes=scratch,
        compiler_params=pltpu.CompilerParams(vmem_limit_bytes=48 * 2**20),
        name=name,
        **rest,
    )


def stay(value):
    return pltpu.with_memory_space_constraint(value, pltpu.HBM)


def shards(embeddings, clusters, priorities):
    rows, width = embeddings.shape
    owners = lax.axis_size(ORDER)
    label_span = rows * owners
    height = owners * (OWN_CAP * width // LANES + META)
    slots = owners * OWN_CAP
    wide = pltpu.VMEM((height, LANES), f32)
    packed, named, rank = call(
        functools.partial(pack_kernel, label_span),
        (
            jax.ShapeDtypeStruct((height, LANES), bf16),
            jax.ShapeDtypeStruct((owners, rows), bf16),
            jax.ShapeDtypeStruct((1, rows), jnp.int32),
        ),
        [
            wide,
            pltpu.VMEM((1, rows), jnp.int32),
            pltpu.VMEM((1, rows), jnp.int32),
            pltpu.VMEM((rows, width), bf16),
            pltpu.SemaphoreType.DMA((2 + X_PIECES,)),
            pltpu.VMEM((slots, rows), bf16),
            pltpu.VMEM((owners, rows), f32),
        ],
        "pack",
        in_specs=[pl.BlockSpec(memory_space=pltpu.HBM)] * 3,
    )(stay(clusters.reshape(1, rows)), stay(priorities.reshape(1, rows)), stay(embeddings))
    arrived = lax.all_to_all(
        packed.reshape(owners, height // owners // 2, 2, LANES),
        ORDER,
        split_axis=0,
        concat_axis=0,
        tiled=True,
    ).reshape(height, LANES)
    result = call(
        functools.partial(score_kernel, label_span),
        jax.ShapeDtypeStruct((owners, OWN_CAP), f32),
        [
            wide,
            pltpu.VMEM((slots, width), bf16),
            pltpu.VMEM((slots, LANES), f32),
            pltpu.VMEM((slots, LANES), f32),
            pltpu.VMEM((slots, LANES), f32),
            pltpu.VMEM((LANES, owners), f32),
            pltpu.VMEM((OWN_CAP * (OWN_CAP + 1) // 2, owners, owners), f32),
            pltpu.VMEM((owners, LANES), f32),
        ],
        "score",
    )(arrived)
    returned = lax.all_to_all(result, ORDER, split_axis=0, concat_axis=0, tiled=True)
    best = call(pick_kernel, jax.ShapeDtypeStruct((1, rows), f32), [], "pick")(returned, named, rank)
    return best.reshape(rows)


def solution(mesh):
    fine = Mesh(mesh.devices.reshape(-1, *PLACE, mesh.shape["gy"]), AXES)
    in_specs = (P(AXES, None), P(AXES), P(AXES))
    return jax.shard_map(shards, mesh=fine, in_specs=in_specs, out_specs=P(AXES), check_vma=False)
```
